32 devices in a mesh: grp: 2 (over y), dev: 16 (over z, x, core).
Axes of the slice: x: 2, y: 2, z: 4, core: 2. Of those that a mesh axis runs over, the one named last changes fastest.
Arguments:
- reservoir: bfloat16 [32768, 1024], P(('grp', 'dev')), may hold values from -6 to 6
- send_rows: int32 [32, 2, 16], P(('grp', 'dev')), may hold values from 0 to 1023
- send_count: int32 [32, 2], P(('grp', 'dev')), may hold values from 0 to 16, as said below
- new_rows: bfloat16 [16384, 1024], P(('grp', 'dev')), may hold values from -6 to 6
- w_up: bfloat16 [1024, 2048], P('dev'), may hold values from -0.1875 to 0.1875
- w_down: bfloat16 [2048, 1024], P('dev'), may hold values from -0.125 to 0.125
- ln_gain: bfloat16 [1024], replicated, may hold values from 0.099609375 to 1.8984375
- grad_new: bfloat16 [16384, 1024], P(('grp', 'dev')), may hold values from -0.046875 to 0.046875
- grad_old: bfloat16 [1024, 1024], P(('grp', 'dev')), may hold values from -0.046875 to 0.046875
Outputs:
- block_out: bfloat16 [16384, 1024], P(('grp', 'dev'))
- grad_up: float32 [1024, 2048], P('dev')
- grad_down: float32 [2048, 1024], P('dev')
The draws below stay inside these ranges and needn't reach their ends.
Inputs may be any that keep to these rules, and one draw needn't show every extreme that they name: send_count[s, t] slots of source s toward group t are live, the others are empty; 16 is reached in every draw, and about a quarter of the (source, group) pairs carry 8 to 16 live slots, the others 0 to 4.
All inputs are finite; a program needn't handle non-finite values.
Results may differ from the reference program's by a relative error of at most 0.024.
Values may be sent and summed in bfloat16 or wider, within the bound.
A program may use at most 64 MiB of HBM per device.

```python
import jax
import jax.numpy as jnp
from jax import lax

D = 1024
HID = 2048
NEW_DEV = 512
CAP = 16
RES_DEV = 1024
TOKENS = 16384
STORED = 32768
OLD = 1024
N_GRP = 2
N_DEV = 16


def draw_send_count(key, part):
    key = jax.random.fold_in(key, 11)
    keys = jax.random.split(key, 4)
    shape = (N_GRP * N_DEV, N_GRP)
    heavy = jax.random.randint(keys[0], shape, 0, 4) == 0
    light_counts = jax.random.randint(keys[1], shape, 0, CAP // 4 + 1)
    heavy_counts = jax.random.randint(keys[2], shape, CAP // 2, CAP + 1)
    counts = jnp.where(heavy, heavy_counts, light_counts).reshape(-1)
    spot = jax.random.randint(keys[3], (), 0, N_GRP * N_DEV * N_GRP)
    counts = counts.at[spot].set(CAP)
    return counts.reshape(shape).astype(jnp.int32)


def plant(result, own_key, smallest, top_value):
    dims = result.shape
    index_at = [jax.random.randint(jax.random.fold_in(own_key, axis), (), 0, dims[axis]) for axis in range(len(dims))]
    result = result.at[tuple(index_at)].set(smallest)
    longest = dims.index(max(dims))
    index_at[longest] = (index_at[longest] + 1) % dims[longest]
    return result.at[tuple(index_at)].set(top_value)


def steps_of(rng, dims, cuts, least, high):
    gain = 1.0
    for position, blocks in cuts:
        steps = jax.random.uniform(jax.random.fold_in(jax.random.fold_in(rng, 6), position), (blocks,), jnp.float32, least / len(cuts), high / len(cuts))
        gain = gain * jnp.repeat(jnp.exp(steps), dims[position] // blocks).reshape((-1,) + (1,) * (len(dims) - 1 - position))
    return gain


def gaussian(own_key, dims, width, limit, shards=(), held_as=jnp.bfloat16):
    level = steps_of(own_key, dims, shards, -0.22, 0.18) if shards else 1.0
    result = jax.random.normal(own_key, dims, jnp.float32) * width * level
    return jnp.minimum(jnp.maximum(result, -limit), limit).astype(held_as)


def setup_inputs(seed: int = 0) -> dict:
    key_of = jax.random.split(jax.random.key(seed), 10)
    reservoir = gaussian(key_of[0], (STORED, D), 1.0, 6.0, ((0, 32),))
    send_rows = plant(jax.random.randint(key_of[1], (N_GRP * N_DEV, N_GRP, CAP), 0, RES_DEV), jax.random.fold_in(key_of[1], 1), 0, RES_DEV - 1).astype(jnp.int32)
    send_count = draw_send_count(jax.random.fold_in(key_of[9], 71), 0)
    new_rows = gaussian(key_of[3], (TOKENS, D), 1.0, 6.0, ((0, 32),))
    w_up = gaussian(key_of[4], (D, HID), D ** -0.5, 0.1875, ((0, 16),))
    w_down = gaussian(key_of[5], (HID, D), HID ** -0.5, 0.125, ((0, 16),))
    ln_gain = jnp.clip(1.0 + 0.18 * jax.random.normal(key_of[6], (D,), jnp.float32), 0.099609375, 1.8984375).astype(jnp.bfloat16)
    grad_new = gaussian(key_of[7], (TOKENS, D), (1.0 / (N_GRP * N_DEV * NEW_DEV) ** 0.5), 0.046875, ((0, 32),))
    grad_old = gaussian(key_of[8], (OLD, D), (1.0 / (N_GRP * N_DEV * NEW_DEV) ** 0.5), 0.046875, ((0, 32),))
    return {"reservoir": reservoir, "send_rows": send_rows, "send_count": send_count, "new_rows": new_rows, "w_up": w_up, "w_down": w_down, "ln_gain": ln_gain, "grad_new": grad_new, "grad_old": grad_old}


def normalize(rows, ln_gain):
    values = rows.astype(jnp.float32)
    center = lax.optimization_barrier(jnp.mean(values, axis=-1, keepdims=True))
    centred = values - center
    spread = lax.optimization_barrier(jnp.mean(centred * centred, axis=-1, keepdims=True))
    return (centred * lax.rsqrt(spread + 1e-05) * ln_gain.astype(jnp.float32)).astype(jnp.bfloat16)

def gelu_parts(pre):
    cdf_value = 0.5 * (1.0 + lax.erf(pre * 0.7071067811865476))
    density = jnp.exp(-0.5 * pre * pre) * 0.3989422804014327
    return (pre * cdf_value, cdf_value + pre * density)

def reference(reservoir, send_rows, send_count, new_rows, w_up, w_down, ln_gain, grad_new, grad_old):
    slot_ids = jnp.arange(CAP, dtype=jnp.int32)
    group_ids = jnp.arange(N_GRP, dtype=jnp.int32)
    old_block = N_GRP * CAP

    def per_device(carry, device):
        target = device // N_DEV
        lane = device % N_DEV
        sources = group_ids * N_DEV + lane
        picks = send_rows[sources, target]
        counts = send_count[sources, target]
        where_rows = (sources[:, None] * RES_DEV + picks).reshape(-1).astype(jnp.int32)
        live = (slot_ids[None, :] < counts[:, None]).astype(jnp.bfloat16).reshape(-1, 1)
        old = reservoir[where_rows] * live
        fresh = lax.dynamic_slice_in_dim(new_rows, (device * NEW_DEV).astype(jnp.int32), NEW_DEV, 0)
        rows = jnp.concatenate([fresh, old], axis=0)
        normed = normalize(rows, ln_gain)
        pre = jnp.dot(normed, w_up, preferred_element_type=jnp.float32)
        act, slope = gelu_parts(pre)
        hidden = act.astype(jnp.bfloat16)
        mixed = jnp.dot(hidden[:NEW_DEV], w_down, preferred_element_type=jnp.float32)
        out_rows = (fresh.astype(jnp.float32) + mixed).astype(jnp.bfloat16)
        cot_new = lax.dynamic_slice_in_dim(grad_new, (device * NEW_DEV).astype(jnp.int32), NEW_DEV, 0)
        cot_old = lax.dynamic_slice_in_dim(grad_old, (device * old_block).astype(jnp.int32), old_block, 0)
        cot = jnp.concatenate([cot_new, cot_old], axis=0)
        back = lax.dot_general(cot, w_down, (((1,), (1,)), ((), ())), preferred_element_type=jnp.float32)
        pre_grad = (back * slope).astype(jnp.bfloat16)
        term_down = lax.dot_general(hidden, cot, (((0,), (0,)), ((), ())), preferred_element_type=jnp.float32)
        term_up = lax.dot_general(normed, pre_grad, (((0,), (0,)), ((), ())), preferred_element_type=jnp.float32)
        term_down = lax.optimization_barrier(term_down.astype(jnp.bfloat16)).astype(jnp.float32)
        term_up = lax.optimization_barrier(term_up.astype(jnp.bfloat16)).astype(jnp.float32)
        return ((carry[0] + term_up, carry[1] + term_down), out_rows)
    start = (jnp.zeros((D, HID), jnp.float32), jnp.zeros((HID, D), jnp.float32))
    devices = jnp.arange(N_GRP * N_DEV, dtype=jnp.int32)
    (grad_up, grad_down), outs = lax.scan(per_device, start, devices)
    return (outs.reshape(N_GRP * N_DEV * NEW_DEV, D), grad_up, grad_down)
```

```python
import jax
import jax.numpy as jnp
from jax import lax
from jax.experimental import pallas as pl
from jax.experimental.pallas import tpu as pltpu
from jax.sharding import PartitionSpec as P


def normalize(rows, ln_gain):
    values = rows.astype(jnp.float32)
    center = jnp.mean(values, axis=-1, keepdims=True)
    centred = values - center
    spread = jnp.mean(centred * centred, axis=-1, keepdims=True)
    return (centred * lax.rsqrt(spread + 1e-05) * ln_gain.astype(jnp.float32)).astype(jnp.bfloat16)


def gelu_parts(pre):
    cdf_value = 0.5 * (1.0 + lax.erf(pre * 0.7071067811865476))
    density = jnp.exp(-0.5 * pre * pre) * 0.3989422804014327
    return (pre * cdf_value, cdf_value + pre * density)


def fetch_old(picked, groups, slots, width):
    return lax.all_to_all(picked, "grp", split_axis=0, concat_axis=0, tiled=True).reshape(
        groups * slots, width
    )


def plain_body(reservoir, send_rows, send_count, new_rows, w_up, w_down, ln_gain, grad_new, grad_old):
    groups = lax.axis_size("grp")
    slots = send_rows.shape[2]
    fresh_count = new_rows.shape[0]
    width = new_rows.shape[1]
    live = (lax.broadcasted_iota(jnp.int32, (groups, slots), 1) < send_count[0][:, None]).astype(
        jnp.bfloat16
    )
    picked = reservoir[send_rows[0].reshape(-1)].reshape(groups, slots, width) * live[:, :, None]
    up_full = lax.all_gather(w_up, "dev", axis=0, tiled=True)
    arrived = fetch_old(picked, groups, slots, width)
    normed = normalize(jnp.concatenate([new_rows, arrived], axis=0), ln_gain)
    pre = jnp.dot(normed, up_full, preferred_element_type=jnp.float32)
    act, slope = gelu_parts(pre)
    hidden = act.astype(jnp.bfloat16)
    fresh_hidden = hidden[:fresh_count]
    cot = jnp.concatenate([grad_new, grad_old], axis=0)
    mixed = jnp.dot(
        fresh_hidden,
        lax.all_gather(w_down, "dev", axis=0, tiled=True),
        preferred_element_type=jnp.float32,
    )
    back = lax.dot_general(
        cot,
        lax.all_gather(w_down, "dev", axis=0, tiled=True),
        (((1,), (1,)), ((), ())),
        preferred_element_type=jnp.float32,
    )
    block_out = (new_rows.astype(jnp.float32) + mixed).astype(jnp.bfloat16)
    pre_grad = (back * slope).astype(jnp.bfloat16)
    group_down = lax.psum_scatter(
        lax.dot_general(
            hidden, cot, (((0,), (0,)), ((), ())), preferred_element_type=jnp.float32
        ).astype(jnp.bfloat16),
        "dev",
        scatter_dimension=0,
        tiled=True,
    )
    group_up = lax.psum_scatter(
        lax.dot_general(
            normed, pre_grad, (((0,), (0,)), ((), ())), preferred_element_type=jnp.float32
        ).astype(jnp.bfloat16),
        "dev",
        scatter_dimension=0,
        tiled=True,
    )
    grad_up, grad_down = (
        lax.psum(group_up, "grp").astype(jnp.float32),
        lax.psum(group_down, "grp").astype(jnp.float32),
    )
    return (block_out, grad_up, grad_down)


FUSED_GROUPS = 2
FUSED_LANES = 16
X_FIRST = (3, 1)
MESH = pl.DeviceIdType.MESH
F32 = jnp.float32
BF16 = jnp.bfloat16


def fused_kernel(
    pick_ref, w_ref, gain_ref, reservoir_hbm, new_hbm, grad_new_hbm, grad_old_hbm,
    out_ref, up_ref, down_ref,
    weights, stored, fresh, cot, picked, arrived, normed, pre, back, hidden, pre_grad,
    terms, from_core, from_x2, from_y, from_x, from_z, final,
    local_sem, send_sem, w_sem, old_send, old_recv, core_sem, x2_sem, y_sem, x_sem, z_sem, final_sem,
):
    y = lax.axis_index("grp")
    lane = lax.axis_index("dev")
    z, x, c = lane // 4, (lane // 2) % 2, lane % 2
    other = 1 - y
    z_of = (z, z + 1 - 2 * (z % 2), (z + 2) % 4, 3 - z)

    def lane_of(k, side, flip):
        xx = x if side == 0 else 1 - x
        cc = c if flip == 0 else 1 - c
        return (z_of[k] * 2 + xx) * 2 + cc

    to_core = {"dev": lane_of(0, 0, 1)}
    to_x = {"dev": lane_of(0, 1, 0)}
    to_y = {"grp": other}
    to_z = (None,) + tuple({"dev": lane_of(k, 0, 0)} for k in (1, 2, 3))
    pending = []

    def send(src, dst, recv, target):
        copy = pltpu.make_async_remote_copy(
            src_ref=src, dst_ref=dst, send_sem=send_sem.at[len(pending)], recv_sem=recv,
            device_id=target, device_id_type=MESH,
        )
        copy.start()
        pending.append(copy)

    def arrive(dst, recv):
        pltpu.make_async_remote_copy(
            src_ref=dst, dst_ref=dst, send_sem=send_sem.at[0], recv_sem=recv,
            device_id=to_core, device_id_type=MESH,
        ).wait_recv()

    new_count = fresh.shape[0]
    rows = cot.shape[0]
    width = cot.shape[1]
    local = [
        pltpu.make_async_copy(reservoir_hbm, stored, local_sem.at[0]),
        pltpu.make_async_copy(new_hbm, fresh, local_sem.at[1]),
        pltpu.make_async_copy(grad_new_hbm, cot.at[pl.ds(0, new_count)], local_sem.at[2]),
        pltpu.make_async_copy(grad_old_hbm, cot.at[pl.ds(new_count, rows - new_count)], local_sem.at[3]),
    ]
    for copy in local:
        copy.start()

    barrier = pltpu.get_barrier_semaphore()
    for target in (to_core, to_x, to_y) + to_z[1:]:
        pl.semaphore_signal(barrier, inc=1, device_id=target, device_id_type=MESH)
    pl.semaphore_wait(barrier, 6)

    def w_send(m, l, target, own=False):
        send(w_ref.at[m] if own else weights.at[m, l], weights.at[m, l], w_sem.at[m, l], target)

    def w_wait(m, l):
        arrive(weights.at[m, l], w_sem.at[m, l])

    w_send(y, lane, to_z[2], True)
    w_send(y, lane, to_z[3], True)
    for m in (y, other):
        w_send(m, lane, to_x, True)
        w_send(m, lane, to_z[1], True)
    for m in (0, 1):
        w_send(m, lane, to_core, True)
    for m in (0, 1):
        weights[m, lane] = w_ref[m]

    local[0].wait()
    hot = (lax.broadcasted_iota(jnp.int32, (pick_ref.shape[0], stored.shape[0]), 1) == pick_ref[...])
    hot = hot.astype(F32).astype(BF16)
    chosen = jnp.dot(hot, stored[...], preferred_element_type=F32).astype(BF16)
    slots = pick_ref.shape[0] // 2
    picked[0] = chosen[:slots]
    picked[1] = chosen[slots:]
    old_copy = pltpu.make_async_remote_copy(
        src_ref=picked.at[other], dst_ref=arrived.at[y], send_sem=old_send, recv_sem=old_recv,
        device_id=to_y, device_id_type=MESH,
    )
    old_copy.start()
    arrived[y] = picked[y]

    def norm(values):
        values = values.astype(F32)
        centred = values - jnp.mean(values, axis=-1, keepdims=True)
        spread = jnp.mean(centred * centred, axis=-1, keepdims=True)
        return (centred * lax.rsqrt(spread + 1e-05) * gain_ref[...].astype(F32)).astype(BF16)

    local[1].wait()

    @pl.loop(0, new_count // 32)
    def _(i):
        at = pl.ds(pl.multiple_of(i * 32, 32), 32)
        normed[at] = norm(fresh[at])

    old_copy.wait()
    for g in (0, 1):
        normed[pl.ds(new_count + g * slots, slots)] = norm(arrived[g])
    local[2].wait()
    local[3].wait()

    def pass_on(m, k, side, targets):
        l = lane_of(k, side, 0)
        w_wait(m, l)
        for target in targets:
            w_send(m, l, target)

    def slab(k, first):
        for m in (0, 1):
            for side in (0, 1):
                w_wait(m, lane_of(k, side, 1))
        zk = z_of[k]
        depth = width // 4
        part = normed[:, pl.ds(pl.multiple_of(zk * depth, depth), depth)]
        half_rows = width // 16
        for half in (0, 1):
            @pl.loop(0, width // 256)
            def _(n):
                at = pl.ds(pl.multiple_of(n * 256, 256), 256)
                to = pl.ds(pl.multiple_of(half * width + n * 256, 256), 256)
                block = weights[0, pl.ds(zk * 4, 4), pl.ds(half * half_rows, half_rows), at]
                got = jnp.dot(part, block.reshape(depth, 256), preferred_element_type=F32)
                if first:
                    pre[:, to] = got
                else:
                    pre[:, to] = pre[:, to] + got

        @pl.loop(0, 2)
        def _(n):
            block = weights[1, pl.ds(zk * 4 + n * 2, 2)].reshape(width // 4, width)
            to = pl.ds(pl.multiple_of(zk * (width // 2) + n * (width // 4), 256), width // 4)
            back[:, to] = lax.dot_general(
                cot[...], block, (((1,), (1,)), ((), ())), preferred_element_type=F32
            )

    for m in (0, 1):
        pass_on(m, 0, 1, (to_core,))
    pass_on(y, 1, 0, (to_x, to_core))
    pass_on(other, 1, 0, (to_core,))
    pass_on(y, 3, 0, (to_x, to_y, to_core))
    slab(0, True)
    pass_on(y, 2, 0, (to_x, to_y, to_core))
    pass_on(y, 1, 1, (to_y, to_core))
    pass_on(other, 3, 0, (to_core,))
    pass_on(y, 3, 1, (to_y, to_core))
    pass_on(other, 2, 0, (to_core,))
    pass_on(other, 1, 1, (to_core,))
    slab(1, False)
    pass_on(y, 2, 1, (to_y, to_core))
    pass_on(other, 3, 1, (to_core,))
    slab(3, False)
    pass_on(other, 2, 1, (to_core,))
    slab(2, False)

    @pl.loop(0, rows // 32)
    def _(i):
        at = pl.ds(pl.multiple_of(i * 32, 32), 32)

        @pl.loop(0, 2 * width // 512)
        def _(j):
            to = pl.ds(pl.multiple_of(j * 512, 512), 512)
            act, slope = gelu_parts(pre[at, to])
            hidden[at, to] = act.astype(BF16)
            pre_grad[at, to] = (back[at, to] * slope).astype(BF16)

    def term_slab(k):
        zk = z_of[k]
        depth = width // 2

        @pl.loop(0, 2)
        def _(n):
            own = hidden[:, pl.ds(pl.multiple_of(zk * depth + n * 256, 256), 256)]
            got = lax.dot_general(own, cot[...], (((0,), (0,)), ((), ())), preferred_element_type=F32)
            terms[1, pl.ds(zk * 4 + n * 2, 2)] = got.astype(BF16).reshape(2, width // 8, width)

        deep = width // 4
        part = normed[:, pl.ds(pl.multiple_of(zk * deep, deep), deep)]
        half_rows = width // 16
        for half in (0, 1):
            @pl.loop(0, 2)
            def _(n):
                to = pl.ds(pl.multiple_of(half * width + n * 512, 512), 512)
                got = lax.dot_general(part, pre_grad[:, to], (((0,), (0,)), ((), ())), preferred_element_type=F32)
                at = pl.ds(pl.multiple_of(n * 512, 512), 512)
                terms[0, pl.ds(zk * 4, 4), pl.ds(half * half_rows, half_rows), at] = (
                    got.astype(BF16).reshape(4, half_rows, 512)
                )
        for side in (1, 0):
            for m in (0, 1):
                send(terms.at[m, lane_of(k, side, 1)], from_core.at[m, k, side], core_sem.at[m, k, side], to_core)

    def add(dst, *parts):
        @pl.loop(0, dst.shape[0] // 32)
        def _(i):
            at = pl.ds(pl.multiple_of(i * 32, 32), 32)
            total = parts[0][at].astype(F32)
            for part in parts[1:]:
                total = total + part[at].astype(F32)
            dst[at] = total.astype(dst.dtype)

    def chip_sum(k, side):
        l = lane_of(k, side, 0)
        for m in (0, 1):
            arrive(from_core.at[m, k, side], core_sem.at[m, k, side])
            parts = [terms.at[m, l], from_core.at[m, k, side]]
            if side == 0 and k in X_FIRST:
                arrive(from_x2.at[m, k], x2_sem.at[m, k])
                parts.append(from_x2.at[m, k])
            add(from_core.at[m, k, side], *parts)
            if side == 1 and k in X_FIRST:
                send(from_core.at[m, k, side], from_x2.at[m, k], x2_sem.at[m, k], to_x)
        if side == 0 or k not in X_FIRST:
            send(from_core.at[other, k, side], from_y.at[k, side], y_sem.at[k, side], to_y)

    def pair_sum(k, side):
        arrive(from_y.at[k, side], y_sem.at[k, side])
        parts = [from_core.at[y, k, side], from_y.at[k, side]]
        if side == 0 and k not in X_FIRST:
            arrive(from_x.at[k], x_sem.at[k])
            parts.append(from_x.at[k])
        if side == 0 and k == 0:
            for j in (1, 2, 3):
                arrive(from_z.at[j], z_sem.at[j])
                parts.append(from_z.at[j])
            add(final.at[y], *parts)
            send(final.at[y], final.at[y], final_sem, to_y)
            return
        add(from_y.at[k, side], *parts)
        if side == 1:
            send(from_y.at[k, side], from_x.at[k], x_sem.at[k], to_x)
        else:
            send(from_y.at[k, side], from_z.at[k], z_sem.at[k], to_z[k])

    def mix(n):
        at = pl.ds(n * 256, 256)
        block = weights[1, :, :, at].reshape(2 * width, 256)
        got = jnp.dot(hidden[pl.ds(0, new_count)], block, preferred_element_type=F32)
        out_ref[:, at] = (fresh[:, at].astype(F32) + got).astype(BF16)

    term_slab(2)
    term_slab(3)
    chip_sum(2, 1)
    chip_sum(2, 0)
    chip_sum(3, 1)
    term_slab(1)
    chip_sum(1, 1)
    chip_sum(3, 0)
    term_slab(0)
    chip_sum(0, 1)
    pair_sum(2, 1)
    chip_sum(1, 0)
    chip_sum(0, 0)
    mix(0)
    pair_sum(3, 0)
    mix(1)
    pair_sum(2, 0)
    mix(2)
    pair_sum(0, 1)
    mix(3)
    pair_sum(1, 0)
    pair_sum(0, 0)
    arrive(final.at[other], final_sem)
    half_rows = width // 16
    for half in (0, 1):
        up_ref[:, pl.ds(half * width, width)] = final[0, pl.ds(half * half_rows, half_rows)].astype(F32)
    down_ref[...] = final[1].astype(F32)
    for copy in pending:
        copy.wait_send()


def fused_body(reservoir, send_rows, send_count, new_rows, w_up, w_down, ln_gain, grad_new, grad_old):
    groups, slots = send_rows.shape[1:]
    live = lax.broadcasted_iota(jnp.int32, (groups, slots), 1) < send_count[0][:, None]
    pick = jnp.where(live, send_rows[0], -1).reshape(groups * slots, 1)
    width = new_rows.shape[1]
    hid = w_up.shape[1]
    fresh_count = new_rows.shape[0]
    rows = fresh_count + grad_old.shape[0]
    chunk = w_down.shape[0]
    packed = jnp.stack([jnp.concatenate([w_up[:, :width], w_up[:, width:]], axis=0), w_down])
    vmem = pl.BlockSpec(memory_space=pltpu.VMEM)
    anywhere = pl.BlockSpec(memory_space=pl.ANY)
    dma = pltpu.SemaphoreType.DMA
    return pl.pallas_call(
        fused_kernel,
        out_shape=(
            jax.ShapeDtypeStruct((fresh_count, width), BF16),
            jax.ShapeDtypeStruct(w_up.shape, F32),
            jax.ShapeDtypeStruct(w_down.shape, F32),
        ),
        in_specs=[vmem] * 3 + [anywhere] * 4,
        out_specs=(vmem,) * 3,
        scratch_shapes=[
            pltpu.VMEM((2, FUSED_LANES, chunk, width), BF16),
            pltpu.VMEM(reservoir.shape, BF16),
            pltpu.VMEM((fresh_count, width), BF16),
            pltpu.VMEM((rows, width), BF16),
            pltpu.VMEM((groups, slots, width), BF16),
            pltpu.VMEM((groups, slots, width), BF16),
            pltpu.VMEM((rows, width), BF16),
            pltpu.VMEM((rows, hid), F32),
            pltpu.VMEM((rows, hid), F32),
            pltpu.VMEM((rows, hid), BF16),
            pltpu.VMEM((rows, hid), BF16),
            pltpu.VMEM((2, FUSED_LANES, chunk, width), BF16),
            pltpu.VMEM((2, 4, 2, chunk, width), BF16),
            pltpu.VMEM((2, 4, chunk, width), BF16),
            pltpu.VMEM((4, 2, chunk, width), BF16),
            pltpu.VMEM((4, chunk, width), BF16),
            pltpu.VMEM((4, chunk, width), BF16),
            pltpu.VMEM((2, chunk, width), BF16),
            dma((4,)),
            dma((72,)),
            dma((2, FUSED_LANES)),
            dma(()),
            dma(()),
            dma((2, 4, 2)),
            dma((2, 4)),
            dma((4, 2)),
            dma((4,)),
            dma((4,)),
            dma(()),
        ],
        compiler_params=pltpu.CompilerParams(
            collective_id=0, has_side_effects=True, vmem_limit_bytes=60 * 1024 * 1024
        ),
        cost_estimate=pl.CostEstimate(
            flops=10 * rows * width * hid, bytes_accessed=16 * 1024 * 1024, transcendentals=2 * rows * hid
        ),
    )(pick, packed, ln_gain.reshape(1, width), reservoir, new_rows, grad_new, grad_old)


def solution(mesh):
    fused = mesh.shape["grp"] == FUSED_GROUPS and mesh.shape["dev"] == FUSED_LANES
    return jax.shard_map(
        fused_body if fused else plain_body,
        mesh=mesh,
        in_specs=(
            P(("grp", "dev"), None),
            P(("grp", "dev"), None, None),
            P(("grp", "dev"), None),
            P(("grp", "dev"), None),
            P("dev", None),
            P("dev", None),
            P(),
            P(("grp", "dev"), None),
            P(("grp", "dev"), None),
        ),
        out_specs=(P(("grp", "dev"), None), P("dev", None), P("dev", None)),
        check_vma=False,
    )
```

```python
import jax
import jax.numpy as jnp
from jax import lax
from jax.experimental import pallas as pl
from jax.experimental.pallas import tpu as pltpu
from jax.sharding import PartitionSpec as P


def normalize(rows, ln_gain):
    values = rows.astype(jnp.float32)
    center = jnp.mean(values, axis=-1, keepdims=True)
    centred = values - center
    spread = jnp.mean(centred * centred, axis=-1, keepdims=True)
    return (centred * lax.rsqrt(spread + 1e-05) * ln_gain.astype(jnp.float32)).astype(jnp.bfloat16)


def gelu_parts(pre):
    cdf_value = 0.5 * (1.0 + lax.erf(pre * 0.7071067811865476))
    density = jnp.exp(-0.5 * pre * pre) * 0.3989422804014327
    return (pre * cdf_value, cdf_value + pre * density)


def fetch_old(picked, groups, slots, width):
    return lax.all_to_all(picked, "grp", split_axis=0, concat_axis=0, tiled=True).reshape(
        groups * slots, width
    )


def plain_body(reservoir, send_rows, send_count, new_rows, w_up, w_down, ln_gain, grad_new, grad_old):
    groups = lax.axis_size("grp")
    slots = send_rows.shape[2]
    fresh_count = new_rows.shape[0]
    width = new_rows.shape[1]
    live = (lax.broadcasted_iota(jnp.int32, (groups, slots), 1) < send_count[0][:, None]).astype(
        jnp.bfloat16
    )
    picked = reservoir[send_rows[0].reshape(-1)].reshape(groups, slots, width) * live[:, :, None]
    up_full = lax.all_gather(w_up, "dev", axis=0, tiled=True)
    arrived = fetch_old(picked, groups, slots, width)
    normed = normalize(jnp.concatenate([new_rows, arrived], axis=0), ln_gain)
    pre = jnp.dot(normed, up_full, preferred_element_type=jnp.float32)
    act, slope = gelu_parts(pre)
    hidden = act.astype(jnp.bfloat16)
    fresh_hidden = hidden[:fresh_count]
    cot = jnp.concatenate([grad_new, grad_old], axis=0)
    mixed = jnp.dot(
        fresh_hidden,
        lax.all_gather(w_down, "dev", axis=0, tiled=True),
        preferred_element_type=jnp.float32,
    )
    back = lax.dot_general(
        cot,
        lax.all_gather(w_down, "dev", axis=0, tiled=True),
        (((1,), (1,)), ((), ())),
        preferred_element_type=jnp.float32,
    )
    block_out = (new_rows.astype(jnp.float32) + mixed).astype(jnp.bfloat16)
    pre_grad = (back * slope).astype(jnp.bfloat16)
    group_down = lax.psum_scatter(
        lax.dot_general(
            hidden, cot, (((0,), (0,)), ((), ())), preferred_element_type=jnp.float32
        ).astype(jnp.bfloat16),
        "dev",
        scatter_dimension=0,
        tiled=True,
    )
    group_up = lax.psum_scatter(
        lax.dot_general(
            normed, pre_grad, (((0,), (0,)), ((), ())), preferred_element_type=jnp.float32
        ).astype(jnp.bfloat16),
        "dev",
        scatter_dimension=0,
        tiled=True,
    )
    grad_up, grad_down = (
        lax.psum(group_up, "grp").astype(jnp.float32),
        lax.psum(group_down, "grp").astype(jnp.float32),
    )
    return (block_out, grad_up, grad_down)


FUSED_GROUPS = 2
FUSED_LANES = 16
X_FIRST = (3, 1)
MESH = pl.DeviceIdType.MESH
F32 = jnp.float32
BF16 = jnp.bfloat16


def fused_kernel(
    rows_ref, count_ref, gain_ref, w_up_ref, w_down_ref, reservoir_hbm, new_hbm, grad_new_hbm, grad_old_hbm,
    out_ref, up_ref, down_ref,
    weights, stored, fresh, cot, picked, arrived, normed, pre, hidden, pre_grad,
    terms, from_core, from_x2, from_y, from_x, from_z, final,
    local_sem, send_sem, w_sem, old_send, old_recv, core_sem, x2_sem, y_sem, x_sem, z_sem, final_sem,
):
    y = lax.axis_index("grp")
    lane = lax.axis_index("dev")
    z, x, c = lane // 4, (lane // 2) % 2, lane % 2
    other = 1 - y
    z_of = (z, z + 1 - 2 * (z % 2), (z + 2) % 4, 3 - z)

    def lane_of(k, side, flip):
        xx = x if side == 0 else 1 - x
        cc = c if flip == 0 else 1 - c
        return (z_of[k] * 2 + xx) * 2 + cc

    to_core = {"dev": lane_of(0, 0, 1)}
    to_x = {"dev": lane_of(0, 1, 0)}
    to_y = {"grp": other}
    to_z = (None,) + tuple({"dev": lane_of(k, 0, 0)} for k in (1, 2, 3))
    pending = []

    def send(src, dst, recv, target):
        copy = pltpu.make_async_remote_copy(
            src_ref=src, dst_ref=dst, send_sem=send_sem.at[len(pending)], recv_sem=recv,
            device_id=target, device_id_type=MESH,
        )
        copy.start()
        pending.append(copy)

    def arrive(dst, recv):
        pltpu.make_async_remote_copy(
            src_ref=dst, dst_ref=dst, send_sem=send_sem.at[0], recv_sem=recv,
            device_id=to_core, device_id_type=MESH,
        ).wait_recv()

    new_count = fresh.shape[0]
    rows = cot.shape[0]
    width = cot.shape[1]
    part_rows = width // 16
    depth = width // 4

    def half(h):
        return pl.ds(pl.multiple_of(h * part_rows, part_rows), part_rows)

    local = [
        pltpu.make_async_copy(reservoir_hbm, stored, local_sem.at[0]),
        pltpu.make_async_copy(new_hbm, fresh, local_sem.at[1]),
        pltpu.make_async_copy(grad_new_hbm, cot.at[pl.ds(0, new_count)], local_sem.at[2]),
        pltpu.make_async_copy(grad_old_hbm, cot.at[pl.ds(new_count, rows - new_count)], local_sem.at[3]),
    ]
    for copy in local:
        copy.start()
    barrier = pltpu.get_barrier_semaphore()
    for target in (to_core, to_x, to_y) + to_z[1:]:
        pl.semaphore_signal(barrier, inc=1, device_id=target, device_id_type=MESH)
    for h in (0, 1):
        weights[0, lane, pl.ds(h * part_rows, part_rows)] = w_up_ref[:, pl.ds(h * width, width)]
    weights[1, lane] = w_down_ref[...]
    pl.semaphore_wait(barrier, 6)

    def w_send(m, h, l, target):
        piece = weights.at[m, l, half(h)]
        send(piece, piece, w_sem.at[m, h, l], target)

    def w_wait(m, h, l):
        arrive(weights.at[m, l, half(h)], w_sem.at[m, h, l])

    def own_send(m):
        w_send(m, y, lane, to_z[3])
        w_send(m, y, lane, to_z[2])
        for h in (y, other):
            w_send(m, h, lane, to_x)
            w_send(m, h, lane, to_z[1])
        for h in (0, 1):
            w_send(m, h, lane, to_core)

    def pass_on(m, h, k, side, targets):
        l = lane_of(k, side, 0)
        w_wait(m, h, l)
        for target in targets:
            w_send(m, h, l, target)

    def slab_ready(m, k):
        for h in (0, 1):
            for side in (0, 1):
                w_wait(m, h, lane_of(k, side, 1))

    own_send(0)

    slots = rows_ref.shape[2]
    local[0].wait()
    slot_ids = lax.broadcasted_iota(jnp.int32, (1, slots), 1)
    for g in (0, 1):
        live = slot_ids < count_ref[:, g : g + 1]
        pick = jnp.where(live, rows_ref[0, g : g + 1, :], -1)
        hot = lax.broadcasted_iota(jnp.int32, (stored.shape[0], slots), 0) == pick
        picked[g] = lax.dot_general(
            hot.astype(F32).astype(BF16), stored[...], (((0,), (0,)), ((), ())), preferred_element_type=F32
        ).astype(BF16)
    old_copy = pltpu.make_async_remote_copy(
        src_ref=picked.at[other], dst_ref=arrived.at[y], send_sem=old_send, recv_sem=old_recv,
        device_id=to_y, device_id_type=MESH,
    )
    old_copy.start()
    arrived[y] = picked[y]
    gain = gain_ref[...].astype(F32).reshape(1, width)

    def norm(values):
        values = values.astype(F32)
        centred = values - jnp.mean(values, axis=-1, keepdims=True)
        spread = jnp.mean(centred * centred, axis=-1, keepdims=True)
        return (centred * lax.rsqrt(spread + 1e-05) * gain).astype(BF16)

    local[1].wait()

    @pl.loop(0, new_count // 32)
    def _(i):
        at = pl.ds(pl.multiple_of(i * 32, 32), 32)
        normed[at] = norm(fresh[at])

    old_copy.wait()
    for g in (0, 1):
        normed[pl.ds(new_count + g * slots, slots)] = norm(arrived[g])
    local[2].wait()
    local[3].wait()

    def pre_slab(k, first):
        slab_ready(0, k)
        zk = z_of[k]
        part = normed[:, pl.ds(pl.multiple_of(zk * depth, depth), depth)]
        for h in (0, 1):
            @pl.loop(0, width // 512)
            def _(n):
                at = pl.ds(pl.multiple_of(n * 512, 512), 512)
                to = pl.ds(pl.multiple_of(h * width + n * 512, 512), 512)
                block = weights[0, pl.ds(zk * 4, 4), pl.ds(h * part_rows, part_rows), at]
                got = jnp.dot(part, block.reshape(depth, 512), preferred_element_type=F32)
                if first:
                    pre[:, to] = got
                else:
                    pre[:, to] = pre[:, to] + got

    def act_slab(k):
        to = pl.ds(pl.multiple_of(z_of[k] * 2 * depth, 512), 2 * depth)

        @pl.loop(0, rows // 32)
        def _(i):
            at = pl.ds(pl.multiple_of(i * 32, 32), 32)
            act, slope = gelu_parts(pre[at, to])
            hidden[at, to] = act.astype(BF16)
            pre[at, to] = slope

    def back_slab(k):
        slab_ready(1, k)
        zk = z_of[k]

        @pl.loop(0, 2)
        def _(n):
            block = weights[1, pl.ds(zk * 4 + n * 2, 2)].reshape(depth, width)
            to = pl.ds(pl.multiple_of(zk * 2 * depth + n * depth, depth), depth)
            got = lax.dot_general(cot[...], block, (((1,), (1,)), ((), ())), preferred_element_type=F32)
            pre_grad[:, to] = (got * pre[:, to]).astype(BF16)

    def to_partner(m, k):
        for side in (1, 0):
            send(terms.at[m, lane_of(k, side, 1)], from_core.at[m, k, side], core_sem.at[m, k, side], to_core)

    def down_term(k):
        zk = z_of[k]

        @pl.loop(0, 2)
        def _(n):
            own = hidden[:, pl.ds(pl.multiple_of(zk * 2 * depth + n * depth, depth), depth)]
            got = lax.dot_general(own, cot[...], (((0,), (0,)), ((), ())), preferred_element_type=F32)
            terms[1, pl.ds(zk * 4 + n * 2, 2)] = got.astype(BF16).reshape(2, 2 * part_rows, width)

        to_partner(1, k)

    def up_term(k):
        zk = z_of[k]
        part = normed[:, pl.ds(pl.multiple_of(zk * depth, depth), depth)]
        for h in (0, 1):
            @pl.loop(0, 2)
            def _(n):
                to = pl.ds(pl.multiple_of(h * width + n * 512, 512), 512)
                got = lax.dot_general(part, pre_grad[:, to], (((0,), (0,)), ((), ())), preferred_element_type=F32)
                at = pl.ds(pl.multiple_of(n * 512, 512), 512)
                terms[0, pl.ds(zk * 4, 4), pl.ds(h * part_rows, part_rows), at] = (
                    got.astype(BF16).reshape(4, part_rows, 512)
                )
        to_partner(0, k)

    def add(dst, *parts):
        @pl.loop(0, dst.shape[0] // 32)
        def _(i):
            at = pl.ds(pl.multiple_of(i * 32, 32), 32)
            total = parts[0][at].astype(F32)
            for part in parts[1:]:
                total = total + part[at].astype(F32)
            dst[at] = total.astype(dst.dtype)

    def chip_sum(m, k, side):
        mine = from_core.at[m, k, side]
        arrive(mine, core_sem.at[m, k, side])
        parts = [terms.at[m, lane_of(k, side, 0)], mine]
        if side == 0 and k in X_FIRST:
            arrive(from_x2.at[m, k], x2_sem.at[m, k])
            parts.append(from_x2.at[m, k])
        add(mine, *parts)
        if side == 1 and k in X_FIRST:
            send(mine, from_x2.at[m, k], x2_sem.at[m, k], to_x)
        else:
            send(from_core.at[m, k, side, half(other)], from_y.at[m, k, side], y_sem.at[m, k, side], to_y)

    def pair_sum(m, k, side):
        mine = from_y.at[m, k, side]
        arrive(mine, y_sem.at[m, k, side])
        parts = [from_core.at[m, k, side, half(y)], mine]
        if side == 0 and k not in X_FIRST:
            arrive(from_x.at[m, k], x_sem.at[m, k])
            parts.append(from_x.at[m, k])
        if side == 0 and k == 0:
            for j in (1, 2, 3):
                arrive(from_z.at[m, j], z_sem.at[m, j])
                parts.append(from_z.at[m, j])
            done = final.at[m, half(y)]
            add(done, *parts)
            send(done, done, final_sem.at[m], to_y)
            return
        add(mine, *parts)
        if side == 1:
            send(mine, from_x.at[m, k], x_sem.at[m, k], to_x)
        else:
            send(mine, from_z.at[m, k], z_sem.at[m, k], to_z[k])

    def mix(n):
        at = pl.ds(n * 256, 256)
        block = weights[1, :, :, at].reshape(2 * width, 256)
        got = jnp.dot(hidden[pl.ds(0, new_count)], block, preferred_element_type=F32)
        out_ref[:, at] = (fresh[:, at].astype(F32) + got).astype(BF16)

    def near(m):
        for h in (0, 1):
            pass_on(m, h, 0, 1, (to_core,))
        pass_on(m, y, 1, 0, (to_x, to_core))
        pass_on(m, other, 1, 0, (to_core,))

    def far(m):
        pass_on(m, y, 3, 0, (to_x, to_y, to_core))
        pass_on(m, y, 2, 0, (to_x, to_y, to_core))

    def cross(m, k):
        pass_on(m, y, k, 1, (to_y, to_core))

    def swap(m, k, side):
        pass_on(m, other, k, side, (to_core,))

    near(0)
    far(0)
    own_send(1)
    cross(0, 1)
    cross(0, 3)
    swap(0, 3, 0)
    pre_slab(0, True)
    cross(0, 2)
    swap(0, 2, 0)
    swap(0, 1, 1)
    near(1)
    swap(0, 3, 1)
    pre_slab(1, False)
    swap(0, 2, 1)
    far(1)
    pre_slab(3, False)
    cross(1, 1)
    pre_slab(2, False)
    cross(1, 3)
    swap(1, 3, 0)
    act_slab(2)
    down_term(2)
    cross(1, 2)
    swap(1, 2, 0)
    swap(1, 1, 1)
    act_slab(3)
    swap(1, 3, 1)
    swap(1, 2, 1)
    down_term(3)
    chip_sum(1, 2, 1)
    chip_sum(1, 3, 1)
    act_slab(1)
    down_term(1)
    chip_sum(1, 2, 0)
    chip_sum(1, 1, 1)
    act_slab(0)
    down_term(0)
    chip_sum(1, 3, 0)
    pair_sum(1, 2, 1)
    chip_sum(1, 0, 1)
    back_slab(0)
    chip_sum(1, 1, 0)
    chip_sum(1, 0, 0)
    back_slab(1)
    pair_sum(1, 3, 0)
    pair_sum(1, 2, 0)
    back_slab(3)
    pair_sum(1, 0, 1)
    back_slab(2)
    up_term(2)
    pair_sum(1, 1, 0)
    up_term(3)
    chip_sum(0, 2, 1)
    chip_sum(0, 3, 1)
    up_term(1)
    chip_sum(0, 2, 0)
    chip_sum(0, 1, 1)
    up_term(0)
    chip_sum(0, 3, 0)
    pair_sum(0, 2, 1)
    chip_sum(0, 0, 1)
    chip_sum(0, 1, 0)
    chip_sum(0, 0, 0)
    pair_sum(1, 0, 0)
    mix(0)
    pair_sum(0, 3, 0)
    mix(1)
    pair_sum(0, 2, 0)
    pair_sum(0, 0, 1)
    mix(2)
    pair_sum(0, 1, 0)
    mix(3)
    arrive(final.at[1, half(other)], final_sem.at[1])
    down_ref[...] = final[1].astype(F32)
    pair_sum(0, 0, 0)
    arrive(final.at[0, half(other)], final_sem.at[0])
    for h in (0, 1):
        up_ref[:, pl.ds(h * width, width)] = final[0, pl.ds(h * part_rows, part_rows)].astype(F32)
    for copy in pending:
        copy.wait_send()


def fused_body(reservoir, send_rows, send_count, new_rows, w_up, w_down, ln_gain, grad_new, grad_old):
    groups, slots = send_rows.shape[1:]
    fresh_count, width = new_rows.shape
    hid = w_up.shape[1]
    rows = fresh_count + grad_old.shape[0]
    chunk = w_down.shape[0]
    vmem = pl.BlockSpec(memory_space=pltpu.VMEM)
    anywhere = pl.BlockSpec(memory_space=pl.ANY)
    dma = pltpu.SemaphoreType.DMA
    held = lambda *shape: pltpu.VMEM(shape, BF16)
    return pl.pallas_call(
        fused_kernel,
        out_shape=(
            jax.ShapeDtypeStruct((fresh_count, width), BF16),
            jax.ShapeDtypeStruct(w_up.shape, F32),
            jax.ShapeDtypeStruct(w_down.shape, F32),
        ),
        in_specs=[vmem] * 5 + [anywhere] * 4,
        out_specs=(vmem,) * 3,
        scratch_shapes=[
            held(2, FUSED_LANES, chunk, width),
            held(*reservoir.shape),
            held(fresh_count, width),
            held(rows, width),
            held(groups, slots, width),
            held(groups, slots, width),
            held(rows, width),
            pltpu.VMEM((rows, hid), F32),
            held(rows, hid),
            held(rows, hid),
            held(2, FUSED_LANES, chunk, width),
            held(2, 4, 2, chunk, width),
            held(2, 4, chunk, width),
            held(2, 4, 2, chunk // 2, width),
            held(2, 4, chunk // 2, width),
            held(2, 4, chunk // 2, width),
            held(2, chunk, width),
            dma((4,)),
            dma((112,)),
            dma((2, 2, FUSED_LANES)),
            dma(()),
            dma(()),
            dma((2, 4, 2)),
            dma((2, 4)),
            dma((2, 4, 2)),
            dma((2, 4)),
            dma((2, 4)),
            dma((2,)),
        ],
        compiler_params=pltpu.CompilerParams(
            collective_id=0, has_side_effects=True, vmem_limit_bytes=60 * 1024 * 1024
        ),
        cost_estimate=pl.CostEstimate(
            flops=10 * rows * width * hid, bytes_accessed=16 * 1024 * 1024, transcendentals=2 * rows * hid
        ),
    )(send_rows, send_count, ln_gain, w_up, w_down, reservoir, new_rows, grad_new, grad_old)


def solution(mesh):
    fused = mesh.shape["grp"] == FUSED_GROUPS and mesh.shape["dev"] == FUSED_LANES
    return jax.shard_map(
        fused_body if fused else plain_body,
        mesh=mesh,
        in_specs=(
            P(("grp", "dev"), None),
            P(("grp", "dev"), None, None),
            P(("grp", "dev"), None),
            P(("grp", "dev"), None),
            P("dev", None),
            P("dev", None),
            P(),
            P(("grp", "dev"), None),
            P(("grp", "dev"), None),
        ),
        out_specs=(P(("grp", "dev"), None), P("dev", None), P("dev", None)),
        check_vma=False,
    )
```

```python
import jax
import jax.numpy as jnp
from jax import lax
from jax.experimental import pallas as pl
from jax.experimental.pallas import tpu as pltpu
from jax.sharding import PartitionSpec as P


def normalize(rows, ln_gain):
    values = rows.astype(jnp.float32)
    center = jnp.mean(values, axis=-1, keepdims=True)
    centred = values - center
    spread = jnp.mean(centred * centred, axis=-1, keepdims=True)
    return (centred * lax.rsqrt(spread + 1e-05) * ln_gain.astype(jnp.float32)).astype(jnp.bfloat16)


def gelu_parts(pre):
    cdf_value = 0.5 * (1.0 + lax.erf(pre * 0.7071067811865476))
    density = jnp.exp(-0.5 * pre * pre) * 0.3989422804014327
    return (pre * cdf_value, cdf_value + pre * density)


def fetch_old(picked, groups, slots, width):
    return lax.all_to_all(picked, "grp", split_axis=0, concat_axis=0, tiled=True).reshape(
        groups * slots, width
    )


def plain_body(reservoir, send_rows, send_count, new_rows, w_up, w_down, ln_gain, grad_new, grad_old):
    groups = lax.axis_size("grp")
    slots = send_rows.shape[2]
    fresh_count = new_rows.shape[0]
    width = new_rows.shape[1]
    live = (lax.broadcasted_iota(jnp.int32, (groups, slots), 1) < send_count[0][:, None]).astype(
        jnp.bfloat16
    )
    picked = reservoir[send_rows[0].reshape(-1)].reshape(groups, slots, width) * live[:, :, None]
    up_full = lax.all_gather(w_up, "dev", axis=0, tiled=True)
    arrived = fetch_old(picked, groups, slots, width)
    normed = normalize(jnp.concatenate([new_rows, arrived], axis=0), ln_gain)
    pre = jnp.dot(normed, up_full, preferred_element_type=jnp.float32)
    act, slope = gelu_parts(pre)
    hidden = act.astype(jnp.bfloat16)
    fresh_hidden = hidden[:fresh_count]
    cot = jnp.concatenate([grad_new, grad_old], axis=0)
    mixed = jnp.dot(
        fresh_hidden,
        lax.all_gather(w_down, "dev", axis=0, tiled=True),
        preferred_element_type=jnp.float32,
    )
    back = lax.dot_general(
        cot,
        lax.all_gather(w_down, "dev", axis=0, tiled=True),
        (((1,), (1,)), ((), ())),
        preferred_element_type=jnp.float32,
    )
    block_out = (new_rows.astype(jnp.float32) + mixed).astype(jnp.bfloat16)
    pre_grad = (back * slope).astype(jnp.bfloat16)
    group_down = lax.psum_scatter(
        lax.dot_general(
            hidden, cot, (((0,), (0,)), ((), ())), preferred_element_type=jnp.float32
        ).astype(jnp.bfloat16),
        "dev",
        scatter_dimension=0,
        tiled=True,
    )
    group_up = lax.psum_scatter(
        lax.dot_general(
            normed, pre_grad, (((0,), (0,)), ((), ())), preferred_element_type=jnp.float32
        ).astype(jnp.bfloat16),
        "dev",
        scatter_dimension=0,
        tiled=True,
    )
    grad_up, grad_down = (
        lax.psum(group_up, "grp").astype(jnp.float32),
        lax.psum(group_down, "grp").astype(jnp.float32),
    )
    return (block_out, grad_up, grad_down)


FUSED_GROUPS = 2
FUSED_LANES = 16
X_FIRST = (3, 1)
MESH = pl.DeviceIdType.MESH
F32 = jnp.float32
BF16 = jnp.bfloat16


def fused_kernel(
    rows_ref, count_ref, gain_ref, w_up_ref, w_down_ref, reservoir_hbm, new_hbm, grad_new_hbm, grad_old_hbm,
    out_ref, up_ref, down_ref,
    weights, stored, fresh, cot, picked, arrived, normed, pre, hidden, pre_grad, normed_t, hidden_t,
    terms, from_core, from_x2, from_y, from_x, from_z, final,
    local_sem, send_sem, w_sem, old_send, old_recv, core_sem, x2_sem, y_sem, x_sem, z_sem, final_sem,
):
    y = lax.axis_index("grp")
    lane = lax.axis_index("dev")
    z, x, c = lane // 4, (lane // 2) % 2, lane % 2
    other = 1 - y
    z_of = (z, z + 1 - 2 * (z % 2), (z + 2) % 4, 3 - z)

    def lane_of(k, side, flip):
        xx = x if side == 0 else 1 - x
        cc = c if flip == 0 else 1 - c
        return (z_of[k] * 2 + xx) * 2 + cc

    to_core = {"dev": lane_of(0, 0, 1)}
    to_x = {"dev": lane_of(0, 1, 0)}
    to_y = {"grp": other}
    to_z = (None,) + tuple({"dev": lane_of(k, 0, 0)} for k in (1, 2, 3))
    pending = []

    def send(src, dst, recv, target):
        copy = pltpu.make_async_remote_copy(
            src_ref=src, dst_ref=dst, send_sem=send_sem.at[len(pending)], recv_sem=recv,
            device_id=target, device_id_type=MESH,
        )
        copy.start()
        pending.append(copy)

    def arrive(dst, recv):
        pltpu.make_async_remote_copy(
            src_ref=dst, dst_ref=dst, send_sem=send_sem.at[0], recv_sem=recv,
            device_id=to_core, device_id_type=MESH,
        ).wait_recv()

    new_count = fresh.shape[0]
    rows = pre.shape[0]
    width = cot.shape[1]
    part_rows = width // 16
    depth = width // 4

    def half(h):
        return pl.ds(pl.multiple_of(h * part_rows, part_rows), part_rows)

    local = [
        pltpu.make_async_copy(reservoir_hbm, stored, local_sem.at[0]),
        pltpu.make_async_copy(new_hbm, fresh, local_sem.at[1]),
        pltpu.make_async_copy(grad_new_hbm, cot.at[pl.ds(0, new_count)], local_sem.at[2]),
        pltpu.make_async_copy(grad_old_hbm, cot.at[pl.ds(new_count, rows - new_count)], local_sem.at[3]),
    ]
    for copy in local:
        copy.start()
    for held in (cot, normed, hidden, pre_grad):
        held[pl.ds(rows, held.shape[0] - rows)] = jnp.zeros((held.shape[0] - rows, held.shape[1]), BF16)
    barrier = pltpu.get_barrier_semaphore()
    for target in (to_core, to_x, to_y) + to_z[1:]:
        pl.semaphore_signal(barrier, inc=1, device_id=target, device_id_type=MESH)
    for h in (0, 1):
        weights[0, lane, pl.ds(h * part_rows, part_rows)] = w_up_ref[:, pl.ds(h * width, width)]
    weights[1, lane] = w_down_ref[...]
    pl.semaphore_wait(barrier, 6)

    def w_send(m, h, l, target):
        piece = weights.at[m, l, half(h)]
        send(piece, piece, w_sem.at[m, h, l], target)

    def w_wait(m, h, l):
        arrive(weights.at[m, l, half(h)], w_sem.at[m, h, l])

    def own_send(m):
        w_send(m, y, lane, to_z[3])
        w_send(m, y, lane, to_z[2])
        for h in (y, other):
            w_send(m, h, lane, to_x)
            w_send(m, h, lane, to_z[1])
        for h in (0, 1):
            w_send(m, h, lane, to_core)

    def pass_on(m, h, k, side, targets):
        l = lane_of(k, side, 0)
        w_wait(m, h, l)
        for target in targets:
            w_send(m, h, l, target)

    def slab_ready(m, k):
        for h in (0, 1):
            for side in (0, 1):
                w_wait(m, h, lane_of(k, side, 1))

    own_send(0)

    slots = rows_ref.shape[2]
    local[0].wait()
    slot_ids = lax.broadcasted_iota(jnp.int32, (1, slots), 1)
    for g in (0, 1):
        live = slot_ids < count_ref[:, g : g + 1]
        pick = jnp.where(live, rows_ref[0, g : g + 1, :], -1)
        hot = lax.broadcasted_iota(jnp.int32, (stored.shape[0], slots), 0) == pick
        picked[g] = lax.dot_general(
            hot.astype(F32).astype(BF16), stored[...], (((0,), (0,)), ((), ())), preferred_element_type=F32
        ).astype(BF16)
    old_copy = pltpu.make_async_remote_copy(
        src_ref=picked.at[other], dst_ref=arrived.at[y], send_sem=old_send, recv_sem=old_recv,
        device_id=to_y, device_id_type=MESH,
    )
    old_copy.start()
    arrived[y] = picked[y]
    gain = gain_ref[...].astype(F32).reshape(1, width)

    def norm(values):
        values = values.astype(F32)
        centred = values - jnp.mean(values, axis=-1, keepdims=True)
        spread = jnp.mean(centred * centred, axis=-1, keepdims=True)
        return (centred * lax.rsqrt(spread + 1e-05) * gain).astype(BF16)

    local[1].wait()

    @pl.loop(0, new_count // 32)
    def _(i):
        at = pl.ds(pl.multiple_of(i * 32, 32), 32)
        normed[at] = norm(fresh[at])

    old_copy.wait()
    for g in (0, 1):
        normed[pl.ds(new_count + g * slots, slots)] = norm(arrived[g])
    local[2].wait()
    local[3].wait()

    @pl.loop(0, 4)
    def _(i):
        at = pl.ds(pl.multiple_of(i * depth, depth), depth)
        normed_t[at] = normed[:, at].T

    def pre_slab(k, first):
        slab_ready(0, k)
        zk = z_of[k]
        part = normed[pl.ds(0, rows), pl.ds(pl.multiple_of(zk * depth, depth), depth)]
        for h in (0, 1):
            @pl.loop(0, width // 512)
            def _(n):
                at = pl.ds(pl.multiple_of(n * 512, 512), 512)
                to = pl.ds(pl.multiple_of(h * width + n * 512, 512), 512)
                block = weights[0, pl.ds(zk * 4, 4), pl.ds(h * part_rows, part_rows), at]
                got = jnp.dot(part, block.reshape(depth, 512), preferred_element_type=F32)
                if first:
                    pre[:, to] = got
                else:
                    pre[:, to] = pre[:, to] + got

    def act_slab(k):
        to = pl.ds(pl.multiple_of(z_of[k] * 2 * depth, 512), 2 * depth)

        @pl.loop(0, rows // 32)
        def _(i):
            at = pl.ds(pl.multiple_of(i * 32, 32), 32)
            act, slope = gelu_parts(pre[at, to])
            hidden[at, to] = act.astype(BF16)
            pre[at, to] = slope

    def back_slab(k):
        slab_ready(1, k)
        zk = z_of[k]

        @pl.loop(0, 2)
        def _(n):
            block = weights[1, pl.ds(zk * 4 + n * 2, 2)].reshape(depth, width)
            to = pl.ds(pl.multiple_of(zk * 2 * depth + n * depth, depth), depth)
            got = lax.dot_general(cot[pl.ds(0, rows)], block, (((1,), (1,)), ((), ())), preferred_element_type=F32)
            pre_grad[pl.ds(0, rows), to] = (got * pre[:, to]).astype(BF16)

    def to_partner(m, k):
        for side in (1, 0):
            send(terms.at[m, lane_of(k, side, 1)], from_core.at[m, k, side], core_sem.at[m, k, side], to_core)

    def down_term(k):
        zk = z_of[k]
        hidden_t[...] = hidden[:, pl.ds(pl.multiple_of(zk * 2 * depth, depth), 2 * depth)].T

        @pl.loop(0, width // 256)
        def _(n):
            at = pl.ds(pl.multiple_of(n * 256, 256), 256)
            got = jnp.dot(hidden_t[...], cot[:, at], preferred_element_type=F32)
            terms[1, pl.ds(zk * 4, 4), :, at] = got.astype(BF16).reshape(4, 2 * part_rows, 256)

        to_partner(1, k)

    def up_term(k):
        zk = z_of[k]
        own = pl.ds(pl.multiple_of(zk * depth, depth), depth)
        for h in (0, 1):
            @pl.loop(0, width // 512)
            def _(n):
                to = pl.ds(pl.multiple_of(h * width + n * 512, 512), 512)
                got = jnp.dot(normed_t[own], pre_grad[:, to], preferred_element_type=F32)
                at = pl.ds(pl.multiple_of(n * 512, 512), 512)
                terms[0, pl.ds(zk * 4, 4), pl.ds(h * part_rows, part_rows), at] = (
                    got.astype(BF16).reshape(4, part_rows, 512)
                )
        to_partner(0, k)

    def add(dst, *parts):
        @pl.loop(0, dst.shape[0] // 32)
        def _(i):
            at = pl.ds(pl.multiple_of(i * 32, 32), 32)
            total = parts[0][at].astype(F32)
            for part in parts[1:]:
                total = total + part[at].astype(F32)
            dst[at] = total.astype(dst.dtype)

    def chip_sum(m, k, side):
        mine = from_core.at[m, k, side]
        arrive(mine, core_sem.at[m, k, side])
        parts = [terms.at[m, lane_of(k, side, 0)], mine]
        if side == 0 and k in X_FIRST:
            arrive(from_x2.at[m, k], x2_sem.at[m, k])
            parts.append(from_x2.at[m, k])
        add(mine, *parts)
        if side == 1 and k in X_FIRST:
            send(mine, from_x2.at[m, k], x2_sem.at[m, k], to_x)
        else:
            send(from_core.at[m, k, side, half(other)], from_y.at[m, k, side], y_sem.at[m, k, side], to_y)

    def pair_sum(m, k, side):
        mine = from_y.at[m, k, side]
        arrive(mine, y_sem.at[m, k, side])
        parts = [from_core.at[m, k, side, half(y)], mine]
        if side == 0 and k not in X_FIRST:
            arrive(from_x.at[m, k], x_sem.at[m, k])
            parts.append(from_x.at[m, k])
        if side == 0 and k == 0:
            for j in (1, 2, 3):
                arrive(from_z.at[m, j], z_sem.at[m, j])
                parts.append(from_z.at[m, j])
            done = final.at[m, half(y)]
            add(done, *parts)
            send(done, done, final_sem.at[m], to_y)
            return
        add(mine, *parts)
        if side == 1:
            send(mine, from_x.at[m, k], x_sem.at[m, k], to_x)
        else:
            send(mine, from_z.at[m, k], z_sem.at[m, k], to_z[k])

    def mix(n):
        at = pl.ds(n * 256, 256)
        block = weights[1, :, :, at].reshape(2 * width, 256)
        got = jnp.dot(hidden[pl.ds(0, new_count)], block, preferred_element_type=F32)
        out_ref[:, at] = (fresh[:, at].astype(F32) + got).astype(BF16)

    def near(m):
        for h in (0, 1):
            pass_on(m, h, 0, 1, (to_core,))
        pass_on(m, y, 1, 0, (to_x, to_core))
        pass_on(m, other, 1, 0, (to_core,))

    def far(m):
        pass_on(m, y, 3, 0, (to_x, to_y, to_core))
        pass_on(m, y, 2, 0, (to_x, to_y, to_core))

    def cross(m, k):
        pass_on(m, y, k, 1, (to_y, to_core))

    def swap(m, k, side):
        pass_on(m, other, k, side, (to_core,))

    near(0)
    far(0)
    own_send(1)
    cross(0, 1)
    cross(0, 3)
    swap(0, 3, 0)
    pre_slab(0, True)
    cross(0, 2)
    swap(0, 2, 0)
    swap(0, 1, 1)
    near(1)
    swap(0, 3, 1)
    pre_slab(1, False)
    swap(0, 2, 1)
    far(1)
    pre_slab(3, False)
    cross(1, 1)
    pre_slab(2, False)
    cross(1, 3)
    swap(1, 3, 0)
    act_slab(2)
    down_term(2)
    cross(1, 2)
    swap(1, 2, 0)
    swap(1, 1, 1)
    act_slab(3)
    swap(1, 3, 1)
    swap(1, 2, 1)
    down_term(3)
    chip_sum(1, 2, 1)
    chip_sum(1, 3, 1)
    act_slab(1)
    down_term(1)
    chip_sum(1, 2, 0)
    chip_sum(1, 1, 1)
    act_slab(0)
    down_term(0)
    chip_sum(1, 3, 0)
    pair_sum(1, 2, 1)
    chip_sum(1, 0, 1)
    back_slab(0)
    chip_sum(1, 1, 0)
    chip_sum(1, 0, 0)
    back_slab(1)
    pair_sum(1, 3, 0)
    pair_sum(1, 2, 0)
    back_slab(3)
    pair_sum(1, 0, 1)
    back_slab(2)
    up_term(2)
    pair_sum(1, 1, 0)
    up_term(3)
    chip_sum(0, 2, 1)
    chip_sum(0, 3, 1)
    up_term(1)
    chip_sum(0, 2, 0)
    chip_sum(0, 1, 1)
    up_term(0)
    chip_sum(0, 0, 1)
    chip_sum(0, 3, 0)
    pair_sum(0, 2, 1)
    chip_sum(0, 0, 0)
    chip_sum(0, 1, 0)
    pair_sum(1, 0, 0)
    mix(0)
    pair_sum(0, 3, 0)
    pair_sum(0, 0, 1)
    mix(1)
    pair_sum(0, 2, 0)
    pair_sum(0, 1, 0)
    mix(2)
    mix(3)
    arrive(final.at[1, half(other)], final_sem.at[1])
    down_ref[...] = final[1].astype(F32)
    pair_sum(0, 0, 0)
    arrive(final.at[0, half(other)], final_sem.at[0])
    for h in (0, 1):
        up_ref[:, pl.ds(h * width, width)] = final[0, pl.ds(h * part_rows, part_rows)].astype(F32)
    for copy in pending:
        copy.wait_send()


def fused_body(reservoir, send_rows, send_count, new_rows, w_up, w_down, ln_gain, grad_new, grad_old):
    groups, slots = send_rows.shape[1:]
    fresh_count, width = new_rows.shape
    hid = w_up.shape[1]
    rows = fresh_count + grad_old.shape[0]
    padded = -(-rows // 128) * 128
    chunk = w_down.shape[0]
    vmem = pl.BlockSpec(memory_space=pltpu.VMEM)
    anywhere = pl.BlockSpec(memory_space=pl.ANY)
    dma = pltpu.SemaphoreType.DMA
    held = lambda *shape: pltpu.VMEM(shape, BF16)
    return pl.pallas_call(
        fused_kernel,
        out_shape=(
            jax.ShapeDtypeStruct((fresh_count, width), BF16),
            jax.ShapeDtypeStruct(w_up.shape, F32),
            jax.ShapeDtypeStruct(w_down.shape, F32),
        ),
        in_specs=[vmem] * 5 + [anywhere] * 4,
        out_specs=(vmem,) * 3,
        scratch_shapes=[
            held(2, FUSED_LANES, chunk, width),
            held(*reservoir.shape),
            held(fresh_count, width),
            held(padded, width),
            held(groups, slots, width),
            held(groups, slots, width),
            held(padded, width),
            pltpu.VMEM((rows, hid), F32),
            held(padded, hid),
            held(padded, hid),
            held(width, padded),
            held(width // 2, padded),
            held(2, FUSED_LANES, chunk, width),
            held(2, 4, 2, chunk, width),
            held(2, 4, chunk, width),
            held(2, 4, 2, chunk // 2, width),
            held(2, 4, chunk // 2, width),
            held(2, 4, chunk // 2, width),
            held(2, chunk, width),
            dma((4,)),
            dma((112,)),
            dma((2, 2, FUSED_LANES)),
            dma(()),
            dma(()),
            dma((2, 4, 2)),
            dma((2, 4)),
            dma((2, 4, 2)),
            dma((2, 4)),
            dma((2, 4)),
            dma((2,)),
        ],
        compiler_params=pltpu.CompilerParams(
            collective_id=0, has_side_effects=True, vmem_limit_bytes=60 * 1024 * 1024
        ),
        cost_estimate=pl.CostEstimate(
            flops=10 * rows * width * hid, bytes_accessed=16 * 1024 * 1024, transcendentals=2 * rows * hid
        ),
    )(send_rows, send_count, ln_gain, w_up, w_down, reservoir, new_rows, grad_new, grad_old)


def solution(mesh):
    fused = mesh.shape["grp"] == FUSED_GROUPS and mesh.shape["dev"] == FUSED_LANES
    return jax.shard_map(
        fused_body if fused else plain_body,
        mesh=mesh,
        in_specs=(
            P(("grp", "dev"), None),
            P(("grp", "dev"), None, None),
            P(("grp", "dev"), None),
            P(("grp", "dev"), None),
            P("dev", None),
            P("dev", None),
            P(),
            P(("grp", "dev"), None),
            P(("grp", "dev"), None),
        ),
        out_specs=(P(("grp", "dev"), None), P("dev", None), P("dev", None)),
        check_vma=False,
    )
```

```python
import jax
import jax.numpy as jnp
from jax import lax
from jax.experimental import pallas as pl
from jax.experimental.pallas import tpu as pltpu
from jax.sharding import PartitionSpec as P


def normalize(rows, ln_gain):
    values = rows.astype(jnp.float32)
    center = jnp.mean(values, axis=-1, keepdims=True)
    centred = values - center
    spread = jnp.mean(centred * centred, axis=-1, keepdims=True)
    return (centred * lax.rsqrt(spread + 1e-05) * ln_gain.astype(jnp.float32)).astype(jnp.bfloat16)


def gelu_parts(pre):
    cdf_value = 0.5 * (1.0 + lax.erf(pre * 0.7071067811865476))
    density = jnp.exp(-0.5 * pre * pre) * 0.3989422804014327
    return (pre * cdf_value, cdf_value + pre * density)


def fetch_old(picked, groups, slots, width):
    return lax.all_to_all(picked, "grp", split_axis=0, concat_axis=0, tiled=True).reshape(
        groups * slots, width
    )


def plain_body(reservoir, send_rows, send_count, new_rows, w_up, w_down, ln_gain, grad_new, grad_old):
    groups = lax.axis_size("grp")
    slots = send_rows.shape[2]
    fresh_count = new_rows.shape[0]
    width = new_rows.shape[1]
    live = (lax.broadcasted_iota(jnp.int32, (groups, slots), 1) < send_count[0][:, None]).astype(
        jnp.bfloat16
    )
    picked = reservoir[send_rows[0].reshape(-1)].reshape(groups, slots, width) * live[:, :, None]
    up_full = lax.all_gather(w_up, "dev", axis=0, tiled=True)
    arrived = fetch_old(picked, groups, slots, width)
    normed = normalize(jnp.concatenate([new_rows, arrived], axis=0), ln_gain)
    pre = jnp.dot(normed, up_full, preferred_element_type=jnp.float32)
    act, slope = gelu_parts(pre)
    hidden = act.astype(jnp.bfloat16)
    fresh_hidden = hidden[:fresh_count]
    cot = jnp.concatenate([grad_new, grad_old], axis=0)
    mixed = jnp.dot(
        fresh_hidden,
        lax.all_gather(w_down, "dev", axis=0, tiled=True),
        preferred_element_type=jnp.float32,
    )
    back = lax.dot_general(
        cot,
        lax.all_gather(w_down, "dev", axis=0, tiled=True),
        (((1,), (1,)), ((), ())),
        preferred_element_type=jnp.float32,
    )
    block_out = (new_rows.astype(jnp.float32) + mixed).astype(jnp.bfloat16)
    pre_grad = (back * slope).astype(jnp.bfloat16)
    group_down = lax.psum_scatter(
        lax.dot_general(
            hidden, cot, (((0,), (0,)), ((), ())), preferred_element_type=jnp.float32
        ).astype(jnp.bfloat16),
        "dev",
        scatter_dimension=0,
        tiled=True,
    )
    group_up = lax.psum_scatter(
        lax.dot_general(
            normed, pre_grad, (((0,), (0,)), ((), ())), preferred_element_type=jnp.float32
        ).astype(jnp.bfloat16),
        "dev",
        scatter_dimension=0,
        tiled=True,
    )
    grad_up, grad_down = (
        lax.psum(group_up, "grp").astype(jnp.float32),
        lax.psum(group_down, "grp").astype(jnp.float32),
    )
    return (block_out, grad_up, grad_down)


FUSED_GROUPS = 2
FUSED_LANES = 16
X_FIRST = (3, 1)
MESH = pl.DeviceIdType.MESH
F32 = jnp.float32
BF16 = jnp.bfloat16


def fused_kernel(
    rows_ref, count_ref, gain_ref, w_up_ref, w_down_ref, reservoir_hbm, new_hbm, grad_new_hbm, grad_old_hbm,
    out_ref, up_ref, down_ref,
    weights, stored, fresh, cot, picked, arrived, normed, pre, hidden, pre_grad, normed_t, hidden_t,
    terms, from_core, from_x2, from_y, from_x, from_z, final,
    local_sem, send_sem, w_sem, old_send, old_recv, core_sem, x2_sem, y_sem, x_sem, z_sem, final_sem,
):
    y = lax.axis_index("grp")
    lane = lax.axis_index("dev")
    z, x, c = lane // 4, (lane // 2) % 2, lane % 2
    other = 1 - y
    z_of = (z, z + 1 - 2 * (z % 2), (z + 2) % 4, 3 - z)

    def lane_of(k, side, flip):
        xx = x if side == 0 else 1 - x
        cc = c if flip == 0 else 1 - c
        return (z_of[k] * 2 + xx) * 2 + cc

    to_core = {"dev": lane_of(0, 0, 1)}
    to_x = {"dev": lane_of(0, 1, 0)}
    to_y = {"grp": other}
    to_z = (None,) + tuple({"dev": lane_of(k, 0, 0)} for k in (1, 2, 3))
    pending = []

    def send(src, dst, recv, target):
        copy = pltpu.make_async_remote_copy(
            src_ref=src, dst_ref=dst, send_sem=send_sem.at[len(pending)], recv_sem=recv,
            device_id=target, device_id_type=MESH,
        )
        copy.start()
        pending.append(copy)

    def arrive(dst, recv):
        pltpu.make_async_remote_copy(
            src_ref=dst, dst_ref=dst, send_sem=send_sem.at[0], recv_sem=recv,
            device_id=to_core, device_id_type=MESH,
        ).wait_recv()

    new_count = fresh.shape[0]
    rows = pre.shape[0]
    width = cot.shape[1]
    part_rows = width // 16
    depth = width // 4

    def half(h):
        return pl.ds(pl.multiple_of(h * part_rows, part_rows), part_rows)

    local = [
        pltpu.make_async_copy(reservoir_hbm, stored, local_sem.at[0]),
        pltpu.make_async_copy(new_hbm, fresh, local_sem.at[1]),
        pltpu.make_async_copy(grad_new_hbm, cot.at[pl.ds(0, new_count)], local_sem.at[2]),
        pltpu.make_async_copy(grad_old_hbm, cot.at[pl.ds(new_count, rows - new_count)], local_sem.at[3]),
    ]
    for copy in local:
        copy.start()
    for held in (cot, normed, hidden, pre_grad):
        held[pl.ds(rows, held.shape[0] - rows)] = jnp.zeros((held.shape[0] - rows, held.shape[1]), BF16)
    barrier = pltpu.get_barrier_semaphore()
    for target in (to_core, to_x, to_y) + to_z[1:]:
        pl.semaphore_signal(barrier, inc=1, device_id=target, device_id_type=MESH)
    for h in (0, 1):
        weights[0, lane, pl.ds(h * part_rows, part_rows)] = w_up_ref[:, pl.ds(h * width, width)]
    weights[1, lane] = w_down_ref[...]
    pl.semaphore_wait(barrier, 6)

    def w_send(m, h, l, target):
        piece = weights.at[m, l, half(h)]
        send(piece, piece, w_sem.at[m, h, l], target)

    def w_wait(m, h, l):
        arrive(weights.at[m, l, half(h)], w_sem.at[m, h, l])

    def own_send(m):
        w_send(m, y, lane, to_x)
        for k in (3, 2, 1):
            w_send(m, y, lane, to_z[k])
        w_send(m, other, lane, to_z[1])
        for h in (0, 1):
            w_send(m, h, lane, to_core)

    def pass_on(m, h, k, side, targets):
        l = lane_of(k, side, 0)
        w_wait(m, h, l)
        for target in targets:
            w_send(m, h, l, target)

    def slab_ready(m, k):
        for h in (0, 1):
            for side in (0, 1):
                w_wait(m, h, lane_of(k, side, 1))

    def first(m):
        pass_on(m, y, 0, 1, (to_y, to_core))

    def far(m, k):
        pass_on(m, y, k, 0, (to_x, to_y, to_core))

    def beside_z(m):
        pass_on(m, y, 1, 0, (to_x, to_core))
        pass_on(m, other, 1, 0, (to_x, to_core))

    def beside_x(m):
        pass_on(m, y, 1, 1, (to_core,))
        pass_on(m, other, 1, 1, (to_core,))

    def cross(m, k):
        pass_on(m, y, k, 1, (to_y, to_core))

    def swap(m, k, side):
        pass_on(m, other, k, side, (to_core,))

    own_send(0)

    slots = rows_ref.shape[2]
    local[0].wait()
    slot_ids = lax.broadcasted_iota(jnp.int32, (1, slots), 1)
    for g in (0, 1):
        live = slot_ids < count_ref[:, g : g + 1]
        pick = jnp.where(live, rows_ref[0, g : g + 1, :], -1)
        hot = lax.broadcasted_iota(jnp.int32, (stored.shape[0], slots), 0) == pick
        picked[g] = lax.dot_general(
            hot.astype(F32).astype(BF16), stored[...], (((0,), (0,)), ((), ())), preferred_element_type=F32
        ).astype(BF16)
    old_copy = pltpu.make_async_remote_copy(
        src_ref=picked.at[other], dst_ref=arrived.at[y], send_sem=old_send, recv_sem=old_recv,
        device_id=to_y, device_id_type=MESH,
    )
    old_copy.start()
    arrived[y] = picked[y]
    first(0)
    far(0, 3)
    far(0, 2)
    gain = gain_ref[...].astype(F32).reshape(1, width)

    def norm(values):
        values = values.astype(F32)
        centred = values - jnp.mean(values, axis=-1, keepdims=True)
        spread = jnp.mean(centred * centred, axis=-1, keepdims=True)
        return (centred * lax.rsqrt(spread + 1e-05) * gain).astype(BF16)

    local[1].wait()

    @pl.loop(0, new_count // 32)
    def _(i):
        at = pl.ds(pl.multiple_of(i * 32, 32), 32)
        normed[at] = norm(fresh[at])

    old_copy.wait()
    for g in (0, 1):
        normed[pl.ds(new_count + g * slots, slots)] = norm(arrived[g])
    local[2].wait()
    local[3].wait()

    @pl.loop(0, 4)
    def _(i):
        at = pl.ds(pl.multiple_of(i * depth, depth), depth)
        normed_t[at] = normed[:, at].T

    def pre_slab(k, first):
        slab_ready(0, k)
        zk = z_of[k]
        part = normed[pl.ds(0, rows), pl.ds(pl.multiple_of(zk * depth, depth), depth)]
        for h in (0, 1):
            @pl.loop(0, width // 512)
            def _(n):
                at = pl.ds(pl.multiple_of(n * 512, 512), 512)
                to = pl.ds(pl.multiple_of(h * width + n * 512, 512), 512)
                block = weights[0, pl.ds(zk * 4, 4), pl.ds(h * part_rows, part_rows), at]
                got = jnp.dot(part, block.reshape(depth, 512), preferred_element_type=F32)
                if first:
                    pre[:, to] = got
                else:
                    pre[:, to] = pre[:, to] + got

    def act_slab(k):
        to = pl.ds(pl.multiple_of(z_of[k] * 2 * depth, 512), 2 * depth)

        @pl.loop(0, rows // 32)
        def _(i):
            at = pl.ds(pl.multiple_of(i * 32, 32), 32)
            act, slope = gelu_parts(pre[at, to])
            hidden[at, to] = act.astype(BF16)
            pre[at, to] = slope

    def back_slab(k):
        slab_ready(1, k)
        zk = z_of[k]

        @pl.loop(0, 2)
        def _(n):
            block = weights[1, pl.ds(zk * 4 + n * 2, 2)].reshape(depth, width)
            to = pl.ds(pl.multiple_of(zk * 2 * depth + n * depth, depth), depth)
            got = lax.dot_general(cot[pl.ds(0, rows)], block, (((1,), (1,)), ((), ())), preferred_element_type=F32)
            pre_grad[pl.ds(0, rows), to] = (got * pre[:, to]).astype(BF16)

    def to_partner(m, k):
        for side in (1, 0):
            send(terms.at[m, lane_of(k, side, 1)], from_core.at[m, k, side], core_sem.at[m, k, side], to_core)

    def down_term(k):
        zk = z_of[k]
        hidden_t[...] = hidden[:, pl.ds(pl.multiple_of(zk * 2 * depth, depth), 2 * depth)].T

        @pl.loop(0, width // 256)
        def _(n):
            at = pl.ds(pl.multiple_of(n * 256, 256), 256)
            got = jnp.dot(hidden_t[...], cot[:, at], preferred_element_type=F32)
            terms[1, pl.ds(zk * 4, 4), :, at] = got.astype(BF16).reshape(4, 2 * part_rows, 256)

        to_partner(1, k)

    def up_term(k):
        zk = z_of[k]
        own = pl.ds(pl.multiple_of(zk * depth, depth), depth)
        for h in (0, 1):
            @pl.loop(0, width // 512)
            def _(n):
                to = pl.ds(pl.multiple_of(h * width + n * 512, 512), 512)
                got = jnp.dot(normed_t[own], pre_grad[:, to], preferred_element_type=F32)
                at = pl.ds(pl.multiple_of(n * 512, 512), 512)
                terms[0, pl.ds(zk * 4, 4), pl.ds(h * part_rows, part_rows), at] = (
                    got.astype(BF16).reshape(4, part_rows, 512)
                )
        to_partner(0, k)

    def add(dst, *parts):
        @pl.loop(0, dst.shape[0] // 32)
        def _(i):
            at = pl.ds(pl.multiple_of(i * 32, 32), 32)
            total = parts[0][at].astype(F32)
            for part in parts[1:]:
                total = total + part[at].astype(F32)
            dst[at] = total.astype(dst.dtype)

    def chip_sum(m, k, side):
        mine = from_core.at[m, k, side]
        arrive(mine, core_sem.at[m, k, side])
        parts = [terms.at[m, lane_of(k, side, 0)], mine]
        if side == 0 and k in X_FIRST:
            arrive(from_x2.at[m, k], x2_sem.at[m, k])
            parts.append(from_x2.at[m, k])
        add(mine, *parts)
        if side == 1 and k in X_FIRST:
            send(mine, from_x2.at[m, k], x2_sem.at[m, k], to_x)
        else:
            send(from_core.at[m, k, side, half(other)], from_y.at[m, k, side], y_sem.at[m, k, side], to_y)

    def pair_sum(m, k, side):
        mine = from_y.at[m, k, side]
        arrive(mine, y_sem.at[m, k, side])
        parts = [from_core.at[m, k, side, half(y)], mine]
        if side == 0 and k not in X_FIRST:
            arrive(from_x.at[m, k], x_sem.at[m, k])
            parts.append(from_x.at[m, k])
        if side == 0 and k == 0:
            for j in (1, 2, 3):
                arrive(from_z.at[m, j], z_sem.at[m, j])
                parts.append(from_z.at[m, j])
            done = final.at[m, half(y)]
            add(done, *parts)
            send(done, done, final_sem.at[m], to_y)
            return
        add(mine, *parts)
        if side == 1:
            send(mine, from_x.at[m, k], x_sem.at[m, k], to_x)
        else:
            send(mine, from_z.at[m, k], z_sem.at[m, k], to_z[k])

    def mix(n):
        at = pl.ds(n * 256, 256)
        block = weights[1, :, :, at].reshape(2 * width, 256)
        got = jnp.dot(hidden[pl.ds(0, new_count)], block, preferred_element_type=F32)
        out_ref[:, at] = (fresh[:, at].astype(F32) + got).astype(BF16)

    beside_z(0)
    own_send(1)
    swap(0, 0, 1)
    cross(0, 3)
    swap(0, 3, 0)
    cross(0, 2)
    swap(0, 2, 0)
    beside_x(0)
    pre_slab(0, True)
    first(1)
    far(1, 3)
    swap(0, 3, 1)
    swap(0, 2, 1)
    pre_slab(1, False)
    far(1, 2)
    beside_z(1)
    pre_slab(3, False)
    cross(1, 3)
    pre_slab(2, False)
    cross(1, 2)
    act_slab(2)
    beside_x(1)
    swap(1, 0, 1)
    swap(1, 3, 0)
    swap(1, 2, 0)
    down_term(2)
    swap(1, 3, 1)
    swap(1, 2, 1)
    act_slab(3)
    chip_sum(1, 2, 1)
    down_term(3)
    chip_sum(1, 2, 0)
    act_slab(1)
    chip_sum(1, 3, 1)
    down_term(1)
    pair_sum(1, 2, 1)
    act_slab(0)
    chip_sum(1, 1, 1)
    chip_sum(1, 3, 0)
    down_term(0)
    pair_sum(1, 2, 0)
    back_slab(0)
    chip_sum(1, 0, 1)
    chip_sum(1, 1, 0)
    pair_sum(1, 3, 0)
    back_slab(1)
    chip_sum(1, 0, 0)
    pair_sum(1, 0, 1)
    back_slab(3)
    pair_sum(1, 1, 0)
    back_slab(2)
    up_term(2)
    up_term(3)
    chip_sum(0, 2, 1)
    chip_sum(0, 3, 1)
    pair_sum(1, 0, 0)
    up_term(1)
    chip_sum(0, 2, 0)
    pair_sum(0, 2, 1)
    chip_sum(0, 1, 1)
    up_term(0)
    chip_sum(0, 3, 0)
    chip_sum(0, 0, 1)
    pair_sum(0, 2, 0)
    chip_sum(0, 0, 0)
    mix(0)
    chip_sum(0, 1, 0)
    pair_sum(0, 3, 0)
    mix(1)
    pair_sum(0, 0, 1)
    mix(2)
    pair_sum(0, 1, 0)
    mix(3)
    arrive(final.at[1, half(other)], final_sem.at[1])
    down_ref[...] = final[1].astype(F32)
    pair_sum(0, 0, 0)
    arrive(final.at[0, half(other)], final_sem.at[0])
    for h in (0, 1):
        up_ref[:, pl.ds(h * width, width)] = final[0, pl.ds(h * part_rows, part_rows)].astype(F32)
    for copy in pending:
        copy.wait_send()


def fused_body(reservoir, send_rows, send_count, new_rows, w_up, w_down, ln_gain, grad_new, grad_old):
    groups, slots = send_rows.shape[1:]
    fresh_count, width = new_rows.shape
    hid = w_up.shape[1]
    rows = fresh_count + grad_old.shape[0]
    padded = -(-rows // 128) * 128
    chunk = w_down.shape[0]
    vmem = pl.BlockSpec(memory_space=pltpu.VMEM)
    anywhere = pl.BlockSpec(memory_space=pl.ANY)
    dma = pltpu.SemaphoreType.DMA
    held = lambda *shape: pltpu.VMEM(shape, BF16)
    return pl.pallas_call(
        fused_kernel,
        out_shape=(
            jax.ShapeDtypeStruct((fresh_count, width), BF16),
            jax.ShapeDtypeStruct(w_up.shape, F32),
            jax.ShapeDtypeStruct(w_down.shape, F32),
        ),
        in_specs=[vmem] * 5 + [anywhere] * 4,
        out_specs=(vmem,) * 3,
        scratch_shapes=[
            held(2, FUSED_LANES, chunk, width),
            held(*reservoir.shape),
            held(fresh_count, width),
            held(padded, width),
            held(groups, slots, width),
            held(groups, slots, width),
            held(padded, width),
            pltpu.VMEM((rows, hid), F32),
            held(padded, hid),
            held(padded, hid),
            held(width, padded),
            held(width // 2, padded),
            held(2, FUSED_LANES, chunk, width),
            held(2, 4, 2, chunk, width),
            held(2, 4, chunk, width),
            held(2, 4, 2, chunk // 2, width),
            held(2, 4, chunk // 2, width),
            held(2, 4, chunk // 2, width),
            held(2, chunk, width),
            dma((4,)),
            dma((112,)),
            dma((2, 2, FUSED_LANES)),
            dma(()),
            dma(()),
            dma((2, 4, 2)),
            dma((2, 4)),
            dma((2, 4, 2)),
            dma((2, 4)),
            dma((2, 4)),
            dma((2,)),
        ],
        compiler_params=pltpu.CompilerParams(
            collective_id=0, has_side_effects=True, vmem_limit_bytes=60 * 1024 * 1024
        ),
        cost_estimate=pl.CostEstimate(
            flops=10 * rows * width * hid, bytes_accessed=16 * 1024 * 1024, transcendentals=2 * rows * hid
        ),
    )(send_rows, send_count, ln_gain, w_up, w_down, reservoir, new_rows, grad_new, grad_old)


def solution(mesh):
    fused = mesh.shape["grp"] == FUSED_GROUPS and mesh.shape["dev"] == FUSED_LANES
    return jax.shard_map(
        fused_body if fused else plain_body,
        mesh=mesh,
        in_specs=(
            P(("grp", "dev"), None),
            P(("grp", "dev"), None, None),
            P(("grp", "dev"), None),
            P(("grp", "dev"), None),
            P("dev", None),
            P("dev", None),
            P(),
            P(("grp", "dev"), None),
            P(("grp", "dev"), None),
        ),
        out_specs=(P(("grp", "dev"), None), P("dev", None), P("dev", None)),
        check_vma=False,
    )
```

```python
import jax
import jax.numpy as jnp
from jax import lax
from jax.experimental import pallas as pl
from jax.experimental.pallas import tpu as pltpu
from jax.sharding import PartitionSpec as P


def normalize(rows, ln_gain):
    values = rows.astype(jnp.float32)
    center = jnp.mean(values, axis=-1, keepdims=True)
    centred = values - center
    spread = jnp.mean(centred * centred, axis=-1, keepdims=True)
    return (centred * lax.rsqrt(spread + 1e-05) * ln_gain.astype(jnp.float32)).astype(jnp.bfloat16)


def gelu_parts(pre):
    cdf_value = 0.5 * (1.0 + lax.erf(pre * 0.7071067811865476))
    density = jnp.exp(-0.5 * pre * pre) * 0.3989422804014327
    return (pre * cdf_value, cdf_value + pre * density)


def fetch_old(picked, groups, slots, width):
    return lax.all_to_all(picked, "grp", split_axis=0, concat_axis=0, tiled=True).reshape(
        groups * slots, width
    )


def plain_body(reservoir, send_rows, send_count, new_rows, w_up, w_down, ln_gain, grad_new, grad_old):
    groups = lax.axis_size("grp")
    slots = send_rows.shape[2]
    fresh_count = new_rows.shape[0]
    width = new_rows.shape[1]
    live = (lax.broadcasted_iota(jnp.int32, (groups, slots), 1) < send_count[0][:, None]).astype(
        jnp.bfloat16
    )
    picked = reservoir[send_rows[0].reshape(-1)].reshape(groups, slots, width) * live[:, :, None]
    up_full = lax.all_gather(w_up, "dev", axis=0, tiled=True)
    arrived = fetch_old(picked, groups, slots, width)
    normed = normalize(jnp.concatenate([new_rows, arrived], axis=0), ln_gain)
    pre = jnp.dot(normed, up_full, preferred_element_type=jnp.float32)
    act, slope = gelu_parts(pre)
    hidden = act.astype(jnp.bfloat16)
    fresh_hidden = hidden[:fresh_count]
    cot = jnp.concatenate([grad_new, grad_old], axis=0)
    mixed = jnp.dot(
        fresh_hidden,
        lax.all_gather(w_down, "dev", axis=0, tiled=True),
        preferred_element_type=jnp.float32,
    )
    back = lax.dot_general(
        cot,
        lax.all_gather(w_down, "dev", axis=0, tiled=True),
        (((1,), (1,)), ((), ())),
        preferred_element_type=jnp.float32,
    )
    block_out = (new_rows.astype(jnp.float32) + mixed).astype(jnp.bfloat16)
    pre_grad = (back * slope).astype(jnp.bfloat16)
    group_down = lax.psum_scatter(
        lax.dot_general(
            hidden, cot, (((0,), (0,)), ((), ())), preferred_element_type=jnp.float32
        ).astype(jnp.bfloat16),
        "dev",
        scatter_dimension=0,
        tiled=True,
    )
    group_up = lax.psum_scatter(
        lax.dot_general(
            normed, pre_grad, (((0,), (0,)), ((), ())), preferred_element_type=jnp.float32
        ).astype(jnp.bfloat16),
        "dev",
        scatter_dimension=0,
        tiled=True,
    )
    grad_up, grad_down = (
        lax.psum(group_up, "grp").astype(jnp.float32),
        lax.psum(group_down, "grp").astype(jnp.float32),
    )
    return (block_out, grad_up, grad_down)


FUSED_GROUPS = 2
FUSED_LANES = 16
X_FIRST = (3, 1)
MESH = pl.DeviceIdType.MESH
F32 = jnp.float32
BF16 = jnp.bfloat16


def fused_kernel(
    rows_ref, count_ref, gain_ref, w_up_ref, w_down_ref, reservoir_hbm, new_hbm, grad_new_hbm, grad_old_hbm,
    out_ref, up_ref, down_ref,
    weights, stored, fresh, cot, picked, arrived, normed, pre, hidden, pre_grad, normed_t, hidden_t,
    terms, from_core, from_x2, from_y, from_x, from_z, final,
    local_sem, send_sem, w_sem, old_send, old_recv, core_sem, x2_sem, y_sem, x_sem, z_sem, final_sem,
):
    y = lax.axis_index("grp")
    lane = lax.axis_index("dev")
    z, x, c = lane // 4, (lane // 2) % 2, lane % 2
    other = 1 - y
    z_of = (z, z + 1 - 2 * (z % 2), (z + 2) % 4, 3 - z)

    def lane_of(k, side, flip):
        xx = x if side == 0 else 1 - x
        cc = c if flip == 0 else 1 - c
        return (z_of[k] * 2 + xx) * 2 + cc

    to_core = {"dev": lane_of(0, 0, 1)}
    to_x = {"dev": lane_of(0, 1, 0)}
    to_y = {"grp": other}
    to_z = (None,) + tuple({"dev": lane_of(k, 0, 0)} for k in (1, 2, 3))
    pending = []

    def send(src, dst, recv, target):
        copy = pltpu.make_async_remote_copy(
            src_ref=src, dst_ref=dst, send_sem=send_sem.at[len(pending)], recv_sem=recv,
            device_id=target, device_id_type=MESH,
        )
        copy.start()
        pending.append(copy)

    def arrive(dst, recv):
        pltpu.make_async_remote_copy(
            src_ref=dst, dst_ref=dst, send_sem=send_sem.at[0], recv_sem=recv,
            device_id=to_core, device_id_type=MESH,
        ).wait_recv()

    new_count = fresh.shape[0]
    rows = pre.shape[0]
    width = cot.shape[1]
    part_rows = width // 16
    depth = width // 4

    def half(h):
        return pl.ds(pl.multiple_of(h * part_rows, part_rows), part_rows)

    local = [
        pltpu.make_async_copy(reservoir_hbm, stored, local_sem.at[0]),
        pltpu.make_async_copy(new_hbm, fresh, local_sem.at[1]),
        pltpu.make_async_copy(grad_new_hbm, cot.at[pl.ds(0, new_count)], local_sem.at[2]),
        pltpu.make_async_copy(grad_old_hbm, cot.at[pl.ds(new_count, rows - new_count)], local_sem.at[3]),
    ]
    for copy in local:
        copy.start()
    for held in (cot, normed, hidden, pre_grad):
        held[pl.ds(rows, held.shape[0] - rows)] = jnp.zeros((held.shape[0] - rows, held.shape[1]), BF16)
    barrier = pltpu.get_barrier_semaphore()
    for target in (to_core, to_x, to_y) + to_z[1:]:
        pl.semaphore_signal(barrier, inc=1, device_id=target, device_id_type=MESH)
    for h in (0, 1):
        weights[0, lane, pl.ds(h * part_rows, part_rows)] = w_up_ref[:, pl.ds(h * width, width)]
    weights[1, lane] = w_down_ref[...]
    pl.semaphore_wait(barrier, 6)

    def w_send(m, h, l, target):
        piece = weights.at[m, l, half(h)]
        send(piece, piece, w_sem.at[m, h, l], target)

    def w_wait(m, h, l):
        arrive(weights.at[m, l, half(h)], w_sem.at[m, h, l])

    def own_send(m):
        w_send(m, y, lane, to_z[3])
        w_send(m, y, lane, to_z[2])
        for h in (y, other):
            w_send(m, h, lane, to_x)
            w_send(m, h, lane, to_z[1])
        for h in (0, 1):
            w_send(m, h, lane, to_core)

    def pass_on(m, h, k, side, targets):
        l = lane_of(k, side, 0)
        w_wait(m, h, l)
        for target in targets:
            w_send(m, h, l, target)

    def slab_ready(m, k):
        for h in (0, 1):
            for side in (0, 1):
                w_wait(m, h, lane_of(k, side, 1))

    own_send(0)

    slots = rows_ref.shape[2]
    local[0].wait()
    slot_ids = lax.broadcasted_iota(jnp.int32, (1, slots), 1)
    for g in (0, 1):
        live = slot_ids < count_ref[:, g : g + 1]
        pick = jnp.where(live, rows_ref[0, g : g + 1, :], -1)
        hot = lax.broadcasted_iota(jnp.int32, (stored.shape[0], slots), 0) == pick
        picked[g] = lax.dot_general(
            hot.astype(F32).astype(BF16), stored[...], (((0,), (0,)), ((), ())), preferred_element_type=F32
        ).astype(BF16)
    old_copy = pltpu.make_async_remote_copy(
        src_ref=picked.at[other], dst_ref=arrived.at[y], send_sem=old_send, recv_sem=old_recv,
        device_id=to_y, device_id_type=MESH,
    )
    old_copy.start()
    arrived[y] = picked[y]
    gain = gain_ref[...].astype(F32).reshape(1, width)

    def norm(values):
        values = values.astype(F32)
        centred = values - jnp.mean(values, axis=-1, keepdims=True)
        spread = jnp.mean(centred * centred, axis=-1, keepdims=True)
        return (centred * lax.rsqrt(spread + 1e-05) * gain).astype(BF16)

    local[1].wait()

    @pl.loop(0, new_count // 32)
    def _(i):
        at = pl.ds(pl.multiple_of(i * 32, 32), 32)
        normed[at] = norm(fresh[at])

    old_copy.wait()
    for g in (0, 1):
        normed[pl.ds(new_count + g * slots, slots)] = norm(arrived[g])
    local[2].wait()
    local[3].wait()

    def pre_slab(k, first):
        slab_ready(0, k)
        zk = z_of[k]
        part = normed[pl.ds(0, rows), pl.ds(pl.multiple_of(zk * depth, depth), depth)]
        for h in (0, 1):
            @pl.loop(0, width // 512)
            def _(n):
                at = pl.ds(pl.multiple_of(n * 512, 512), 512)
                to = pl.ds(pl.multiple_of(h * width + n * 512, 512), 512)
                block = weights[0, pl.ds(zk * 4, 4), pl.ds(h * part_rows, part_rows), at]
                got = jnp.dot(part, block.reshape(depth, 512), preferred_element_type=F32)
                if first:
                    pre[:, to] = got
                else:
                    pre[:, to] = pre[:, to] + got

    def act_slab(k):
        to = pl.ds(pl.multiple_of(z_of[k] * 2 * depth, 512), 2 * depth)

        @pl.loop(0, rows // 32)
        def _(i):
            at = pl.ds(pl.multiple_of(i * 32, 32), 32)
            act, slope = gelu_parts(pre[at, to])
            hidden[at, to] = act.astype(BF16)
            pre[at, to] = slope

    def back_slab(k):
        slab_ready(1, k)
        zk = z_of[k]

        @pl.loop(0, 2)
        def _(n):
            block = weights[1, pl.ds(zk * 4 + n * 2, 2)].reshape(depth, width)
            to = pl.ds(pl.multiple_of(zk * 2 * depth + n * depth, depth), depth)
            got = lax.dot_general(cot[pl.ds(0, rows)], block, (((1,), (1,)), ((), ())), preferred_element_type=F32)
            pre_grad[pl.ds(0, rows), to] = (got * pre[:, to]).astype(BF16)

    def to_partner(m, k):
        for side in (1, 0):
            send(terms.at[m, lane_of(k, side, 1)], from_core.at[m, k, side], core_sem.at[m, k, side], to_core)

    def down_term(k, following=None):
        zk = z_of[k]
        hidden_t[...] = hidden[:, pl.ds(pl.multiple_of(zk * 2 * depth, depth), 2 * depth)].T

        @pl.loop(0, width // 256)
        def _(n):
            at = pl.ds(pl.multiple_of(n * 256, 256), 256)
            got = jnp.dot(hidden_t[...], cot[:, at], preferred_element_type=F32)
            if following is not None:
                start = z_of[following] * 2 * depth + n * (depth // 2)
                to = pl.ds(pl.multiple_of(start, depth // 2), depth // 2)
                for i in range(rows // 32):
                    act, slope = gelu_parts(pre[pl.ds(i * 32, 32), to])
                    hidden[pl.ds(i * 32, 32), to] = act.astype(BF16)
                    pre[pl.ds(i * 32, 32), to] = slope
            terms[1, pl.ds(zk * 4, 4), :, at] = got.astype(BF16).reshape(4, 2 * part_rows, 256)

        to_partner(1, k)

    def up_term(k):
        zk = z_of[k]
        own = pl.ds(pl.multiple_of(zk * depth, depth), depth)
        for h in (0, 1):
            @pl.loop(0, width // 512)
            def _(n):
                to = pl.ds(pl.multiple_of(h * width + n * 512, 512), 512)
                got = jnp.dot(normed_t[own], pre_grad[:, to], preferred_element_type=F32)
                at = pl.ds(pl.multiple_of(n * 512, 512), 512)
                terms[0, pl.ds(zk * 4, 4), pl.ds(h * part_rows, part_rows), at] = (
                    got.astype(BF16).reshape(4, part_rows, 512)
                )
        to_partner(0, k)

    def add(dst, *parts):
        @pl.loop(0, dst.shape[0] // 32)
        def _(i):
            at = pl.ds(pl.multiple_of(i * 32, 32), 32)
            total = parts[0][at].astype(F32)
            for part in parts[1:]:
                total = total + part[at].astype(F32)
            dst[at] = total.astype(dst.dtype)

    def chip_sum(m, k, side):
        mine = from_core.at[m, k, side]
        arrive(mine, core_sem.at[m, k, side])
        parts = [terms.at[m, lane_of(k, side, 0)], mine]
        if side == 0 and k in X_FIRST:
            arrive(from_x2.at[m, k], x2_sem.at[m, k])
            parts.append(from_x2.at[m, k])
        add(mine, *parts)
        if side == 1 and k in X_FIRST:
            send(mine, from_x2.at[m, k], x2_sem.at[m, k], to_x)
        else:
            send(from_core.at[m, k, side, half(other)], from_y.at[m, k, side], y_sem.at[m, k, side], to_y)

    def pair_sum(m, k, side):
        mine = from_y.at[m, k, side]
        arrive(mine, y_sem.at[m, k, side])
        parts = [from_core.at[m, k, side, half(y)], mine]
        if side == 0 and k not in X_FIRST:
            arrive(from_x.at[m, k], x_sem.at[m, k])
            parts.append(from_x.at[m, k])
        if side == 0 and k == 0:
            for j in (1, 2, 3):
                arrive(from_z.at[m, j], z_sem.at[m, j])
                parts.append(from_z.at[m, j])
            done = final.at[m, half(y)]
            add(done, *parts)
            send(done, done, final_sem.at[m], to_y)
            return
        add(mine, *parts)
        if side == 1:
            send(mine, from_x.at[m, k], x_sem.at[m, k], to_x)
        else:
            send(mine, from_z.at[m, k], z_sem.at[m, k], to_z[k])

    def mix(n):
        at = pl.ds(n * 256, 256)
        block = weights[1, :, :, at].reshape(2 * width, 256)
        got = jnp.dot(hidden[pl.ds(0, new_count)], block, preferred_element_type=F32)
        out_ref[:, at] = (fresh[:, at].astype(F32) + got).astype(BF16)

    def near(m):
        for h in (0, 1):
            pass_on(m, h, 0, 1, (to_core,))
        pass_on(m, y, 1, 0, (to_x, to_core))
        pass_on(m, other, 1, 0, (to_core,))

    def far(m):
        pass_on(m, y, 3, 0, (to_x, to_y, to_core))
        pass_on(m, y, 2, 0, (to_x, to_y, to_core))

    def cross(m, k):
        pass_on(m, y, k, 1, (to_y, to_core))

    def swap(m, k, side):
        pass_on(m, other, k, side, (to_core,))

    near(0)
    far(0)
    own_send(1)

    @pl.loop(0, 4)
    def _(i):
        at = pl.ds(pl.multiple_of(i * depth, depth), depth)
        normed_t[at] = normed[:, at].T

    cross(0, 1)
    cross(0, 3)
    swap(0, 3, 0)
    pre_slab(0, True)
    cross(0, 2)
    swap(0, 2, 0)
    swap(0, 1, 1)
    near(1)
    swap(0, 3, 1)
    pre_slab(1, False)
    swap(0, 2, 1)
    far(1)
    pre_slab(3, False)
    cross(1, 1)
    pre_slab(2, False)
    cross(1, 3)
    swap(1, 3, 0)
    act_slab(2)
    down_term(2, 3)
    cross(1, 2)
    swap(1, 2, 0)
    swap(1, 1, 1)
    swap(1, 3, 1)
    swap(1, 2, 1)
    down_term(3, 1)
    chip_sum(1, 2, 1)
    chip_sum(1, 3, 1)
    down_term(1, 0)
    chip_sum(1, 2, 0)
    chip_sum(1, 1, 1)
    down_term(0)
    chip_sum(1, 3, 0)
    pair_sum(1, 2, 1)
    chip_sum(1, 0, 1)
    back_slab(0)
    chip_sum(1, 1, 0)
    chip_sum(1, 0, 0)
    back_slab(1)
    pair_sum(1, 3, 0)
    pair_sum(1, 2, 0)
    back_slab(3)
    pair_sum(1, 0, 1)
    back_slab(2)
    up_term(2)
    pair_sum(1, 1, 0)
    up_term(3)
    chip_sum(0, 2, 1)
    chip_sum(0, 3, 1)
    up_term(1)
    chip_sum(0, 2, 0)
    chip_sum(0, 1, 1)
    up_term(0)
    chip_sum(0, 0, 1)
    chip_sum(0, 3, 0)
    pair_sum(0, 2, 1)
    chip_sum(0, 0, 0)
    chip_sum(0, 1, 0)
    pair_sum(1, 0, 0)
    mix(0)
    pair_sum(0, 3, 0)
    pair_sum(0, 0, 1)
    mix(1)
    pair_sum(0, 2, 0)
    pair_sum(0, 1, 0)
    mix(2)
    mix(3)
    arrive(final.at[1, half(other)], final_sem.at[1])
    down_ref[...] = final[1].astype(F32)
    pair_sum(0, 0, 0)
    arrive(final.at[0, half(other)], final_sem.at[0])
    for h in (0, 1):
        up_ref[:, pl.ds(h * width, width)] = final[0, pl.ds(h * part_rows, part_rows)].astype(F32)
    for copy in pending:
        copy.wait_send()


def fused_body(reservoir, send_rows, send_count, new_rows, w_up, w_down, ln_gain, grad_new, grad_old):
    groups, slots = send_rows.shape[1:]
    fresh_count, width = new_rows.shape
    hid = w_up.shape[1]
    rows = fresh_count + grad_old.shape[0]
    padded = -(-rows // 128) * 128
    chunk = w_down.shape[0]
    vmem = pl.BlockSpec(memory_space=pltpu.VMEM)
    anywhere = pl.BlockSpec(memory_space=pl.ANY)
    dma = pltpu.SemaphoreType.DMA
    held = lambda *shape: pltpu.VMEM(shape, BF16)
    return pl.pallas_call(
        fused_kernel,
        out_shape=(
            jax.ShapeDtypeStruct((fresh_count, width), BF16),
            jax.ShapeDtypeStruct(w_up.shape, F32),
            jax.ShapeDtypeStruct(w_down.shape, F32),
        ),
        in_specs=[vmem] * 5 + [anywhere] * 4,
        out_specs=(vmem,) * 3,
        scratch_shapes=[
            held(2, FUSED_LANES, chunk, width),
            held(*reservoir.shape),
            held(fresh_count, width),
            held(padded, width),
            held(groups, slots, width),
            held(groups, slots, width),
            held(padded, width),
            pltpu.VMEM((rows, hid), F32),
            held(padded, hid),
            held(padded, hid),
            held(width, padded),
            held(width // 2, padded),
            held(2, FUSED_LANES, chunk, width),
            held(2, 4, 2, chunk, width),
            held(2, 4, chunk, width),
            held(2, 4, 2, chunk // 2, width),
            held(2, 4, chunk // 2, width),
            held(2, 4, chunk // 2, width),
            held(2, chunk, width),
            dma((4,)),
            dma((112,)),
            dma((2, 2, FUSED_LANES)),
            dma(()),
            dma(()),
            dma((2, 4, 2)),
            dma((2, 4)),
            dma((2, 4, 2)),
            dma((2, 4)),
            dma((2, 4)),
            dma((2,)),
        ],
        compiler_params=pltpu.CompilerParams(
            collective_id=0, has_side_effects=True, vmem_limit_bytes=60 * 1024 * 1024
        ),
        cost_estimate=pl.CostEstimate(
            flops=10 * rows * width * hid, bytes_accessed=16 * 1024 * 1024, transcendentals=2 * rows * hid
        ),
    )(send_rows, send_count, ln_gain, w_up, w_down, reservoir, new_rows, grad_new, grad_old)


def solution(mesh):
    fused = mesh.shape["grp"] == FUSED_GROUPS and mesh.shape["dev"] == FUSED_LANES
    return jax.shard_map(
        fused_body if fused else plain_body,
        mesh=mesh,
        in_specs=(
            P(("grp", "dev"), None),
            P(("grp", "dev"), None, None),
            P(("grp", "dev"), None),
            P(("grp", "dev"), None),
            P("dev", None),
            P("dev", None),
            P(),
            P(("grp", "dev"), None),
            P(("grp", "dev"), None),
        ),
        out_specs=(P(("grp", "dev"), None), P("dev", None), P("dev", None)),
        check_vma=False,
    )
```

```python
import jax
import jax.numpy as jnp
from jax import lax
from jax.experimental import pallas as pl
from jax.experimental.pallas import tpu as pltpu
from jax.sharding import PartitionSpec as P


def normalize(rows, ln_gain):
    values = rows.astype(jnp.float32)
    center = jnp.mean(values, axis=-1, keepdims=True)
    centred = values - center
    spread = jnp.mean(centred * centred, axis=-1, keepdims=True)
    return (centred * lax.rsqrt(spread + 1e-05) * ln_gain.astype(jnp.float32)).astype(jnp.bfloat16)


def gelu_parts(pre):
    cdf_value = 0.5 * (1.0 + lax.erf(pre * 0.7071067811865476))
    density = jnp.exp(-0.5 * pre * pre) * 0.3989422804014327
    return (pre * cdf_value, cdf_value + pre * density)


def fetch_old(picked, groups, slots, width):
    return lax.all_to_all(picked, "grp", split_axis=0, concat_axis=0, tiled=True).reshape(
        groups * slots, width
    )


def plain_body(reservoir, send_rows, send_count, new_rows, w_up, w_down, ln_gain, grad_new, grad_old):
    groups = lax.axis_size("grp")
    slots = send_rows.shape[2]
    fresh_count = new_rows.shape[0]
    width = new_rows.shape[1]
    live = (lax.broadcasted_iota(jnp.int32, (groups, slots), 1) < send_count[0][:, None]).astype(
        jnp.bfloat16
    )
    picked = reservoir[send_rows[0].reshape(-1)].reshape(groups, slots, width) * live[:, :, None]
    up_full = lax.all_gather(w_up, "dev", axis=0, tiled=True)
    arrived = fetch_old(picked, groups, slots, width)
    normed = normalize(jnp.concatenate([new_rows, arrived], axis=0), ln_gain)
    pre = jnp.dot(normed, up_full, preferred_element_type=jnp.float32)
    act, slope = gelu_parts(pre)
    hidden = act.astype(jnp.bfloat16)
    fresh_hidden = hidden[:fresh_count]
    cot = jnp.concatenate([grad_new, grad_old], axis=0)
    mixed = jnp.dot(
        fresh_hidden,
        lax.all_gather(w_down, "dev", axis=0, tiled=True),
        preferred_element_type=jnp.float32,
    )
    back = lax.dot_general(
        cot,
        lax.all_gather(w_down, "dev", axis=0, tiled=True),
        (((1,), (1,)), ((), ())),
        preferred_element_type=jnp.float32,
    )
    block_out = (new_rows.astype(jnp.float32) + mixed).astype(jnp.bfloat16)
    pre_grad = (back * slope).astype(jnp.bfloat16)
    group_down = lax.psum_scatter(
        lax.dot_general(
            hidden, cot, (((0,), (0,)), ((), ())), preferred_element_type=jnp.float32
        ).astype(jnp.bfloat16),
        "dev",
        scatter_dimension=0,
        tiled=True,
    )
    group_up = lax.psum_scatter(
        lax.dot_general(
            normed, pre_grad, (((0,), (0,)), ((), ())), preferred_element_type=jnp.float32
        ).astype(jnp.bfloat16),
        "dev",
        scatter_dimension=0,
        tiled=True,
    )
    grad_up, grad_down = (
        lax.psum(group_up, "grp").astype(jnp.float32),
        lax.psum(group_down, "grp").astype(jnp.float32),
    )
    return (block_out, grad_up, grad_down)


FUSED_GROUPS = 2
FUSED_LANES = 16
X_FIRST = (3, 1)
MESH = pl.DeviceIdType.MESH
F32 = jnp.float32
BF16 = jnp.bfloat16


def fused_kernel(
    rows_ref, count_ref, gain_ref, w_up_ref, w_down_ref, reservoir_hbm, new_hbm, grad_new_hbm, grad_old_hbm,
    out_ref, up_ref, down_ref,
    weights, stored, fresh, cot, picked, arrived, normed, pre, hidden, pre_grad, normed_t, hidden_t,
    terms, from_core, from_x2, from_y, from_x, from_z, final,
    local_sem, send_sem, w_sem, old_send, old_recv, core_sem, x2_sem, y_sem, x_sem, z_sem, final_sem,
):
    y = lax.axis_index("grp")
    lane = lax.axis_index("dev")
    z, x, c = lane // 4, (lane // 2) % 2, lane % 2
    other = 1 - y
    z_of = (z, z + 1 - 2 * (z % 2), (z + 2) % 4, 3 - z)

    def lane_of(k, side, flip):
        xx = x if side == 0 else 1 - x
        cc = c if flip == 0 else 1 - c
        return (z_of[k] * 2 + xx) * 2 + cc

    to_core = {"dev": lane_of(0, 0, 1)}
    to_x = {"dev": lane_of(0, 1, 0)}
    to_y = {"grp": other}
    to_z = (None,) + tuple({"dev": lane_of(k, 0, 0)} for k in (1, 2, 3))
    pending = []

    def send(src, dst, recv, target):
        copy = pltpu.make_async_remote_copy(
            src_ref=src, dst_ref=dst, send_sem=send_sem.at[len(pending)], recv_sem=recv,
            device_id=target, device_id_type=MESH,
        )
        copy.start()
        pending.append(copy)

    def arrive(dst, recv):
        pltpu.make_async_remote_copy(
            src_ref=dst, dst_ref=dst, send_sem=send_sem.at[0], recv_sem=recv,
            device_id=to_core, device_id_type=MESH,
        ).wait_recv()

    new_count = fresh.shape[0]
    rows = pre.shape[0]
    width = cot.shape[1]
    part_rows = width // 16
    depth = width // 4

    def half(h):
        return pl.ds(pl.multiple_of(h * part_rows, part_rows), part_rows)

    local = [
        pltpu.make_async_copy(reservoir_hbm, stored, local_sem.at[0]),
        pltpu.make_async_copy(new_hbm, fresh, local_sem.at[1]),
        pltpu.make_async_copy(grad_new_hbm, cot.at[pl.ds(0, new_count)], local_sem.at[2]),
        pltpu.make_async_copy(grad_old_hbm, cot.at[pl.ds(new_count, rows - new_count)], local_sem.at[3]),
    ]
    for copy in local:
        copy.start()
    for held in (cot, normed, hidden, pre_grad):
        held[pl.ds(rows, held.shape[0] - rows)] = jnp.zeros((held.shape[0] - rows, held.shape[1]), BF16)
    barrier = pltpu.get_barrier_semaphore()
    for target in (to_core, to_x, to_y) + to_z[1:]:
        pl.semaphore_signal(barrier, inc=1, device_id=target, device_id_type=MESH)
    for h in (0, 1):
        weights[0, lane, pl.ds(h * part_rows, part_rows)] = w_up_ref[:, pl.ds(h * width, width)]
    weights[1, lane] = w_down_ref[...]
    pl.semaphore_wait(barrier, 6)

    def w_send(m, h, l, target):
        piece = weights.at[m, l, half(h)]
        send(piece, piece, w_sem.at[m, h, l], target)

    def w_wait(m, h, l):
        arrive(weights.at[m, l, half(h)], w_sem.at[m, h, l])

    def own_send(m):
        w_send(m, y, lane, to_z[3])
        w_send(m, y, lane, to_z[2])
        w_send(m, other, lane, to_z[2])
        for h in (y, other):
            w_send(m, h, lane, to_x)
            w_send(m, h, lane, to_z[1])
        for h in (0, 1):
            w_send(m, h, lane, to_core)

    def pass_on(m, h, k, side, targets):
        l = lane_of(k, side, 0)
        w_wait(m, h, l)
        for target in targets:
            w_send(m, h, l, target)

    def slab_ready(m, k):
        for h in (0, 1):
            for side in (0, 1):
                w_wait(m, h, lane_of(k, side, 1))

    own_send(0)

    slots = rows_ref.shape[2]
    local[0].wait()
    slot_ids = lax.broadcasted_iota(jnp.int32, (1, slots), 1)
    for g in (0, 1):
        live = slot_ids < count_ref[:, g : g + 1]
        pick = jnp.where(live, rows_ref[0, g : g + 1, :], -1)
        hot = lax.broadcasted_iota(jnp.int32, (stored.shape[0], slots), 0) == pick
        picked[g] = lax.dot_general(
            hot.astype(F32).astype(BF16), stored[...], (((0,), (0,)), ((), ())), preferred_element_type=F32
        ).astype(BF16)
    old_copy = pltpu.make_async_remote_copy(
        src_ref=picked.at[other], dst_ref=arrived.at[y], send_sem=old_send, recv_sem=old_recv,
        device_id=to_y, device_id_type=MESH,
    )
    old_copy.start()
    arrived[y] = picked[y]
    gain = gain_ref[...].astype(F32).reshape(1, width)

    def norm(values):
        values = values.astype(F32)
        centred = values - jnp.mean(values, axis=-1, keepdims=True)
        spread = jnp.mean(centred * centred, axis=-1, keepdims=True)
        return (centred * lax.rsqrt(spread + 1e-05) * gain).astype(BF16)

    local[1].wait()

    @pl.loop(0, new_count // 32)
    def _(i):
        at = pl.ds(pl.multiple_of(i * 32, 32), 32)
        normed[at] = norm(fresh[at])

    old_copy.wait()
    for g in (0, 1):
        normed[pl.ds(new_count + g * slots, slots)] = norm(arrived[g])
    local[2].wait()
    local[3].wait()

    def pre_slab(k, first):
        slab_ready(0, k)
        zk = z_of[k]
        part = normed[pl.ds(0, rows), pl.ds(pl.multiple_of(zk * depth, depth), depth)]
        for h in (0, 1):
            @pl.loop(0, width // 512)
            def _(n):
                at = pl.ds(pl.multiple_of(n * 512, 512), 512)
                to = pl.ds(pl.multiple_of(h * width + n * 512, 512), 512)
                block = weights[0, pl.ds(zk * 4, 4), pl.ds(h * part_rows, part_rows), at]
                got = jnp.dot(part, block.reshape(depth, 512), preferred_element_type=F32)
                if first:
                    pre[:, to] = got
                else:
                    pre[:, to] = pre[:, to] + got

    def act_slab(k):
        to = pl.ds(pl.multiple_of(z_of[k] * 2 * depth, 512), 2 * depth)

        @pl.loop(0, rows // 32)
        def _(i):
            at = pl.ds(pl.multiple_of(i * 32, 32), 32)
            act, slope = gelu_parts(pre[at, to])
            hidden[at, to] = act.astype(BF16)
            pre[at, to] = slope

    def back_slab(k):
        slab_ready(1, k)
        zk = z_of[k]

        @pl.loop(0, 2)
        def _(n):
            block = weights[1, pl.ds(zk * 4 + n * 2, 2)].reshape(depth, width)
            to = pl.ds(pl.multiple_of(zk * 2 * depth + n * depth, depth), depth)
            got = lax.dot_general(cot[pl.ds(0, rows)], block, (((1,), (1,)), ((), ())), preferred_element_type=F32)
            pre_grad[pl.ds(0, rows), to] = (got * pre[:, to]).astype(BF16)

    def to_partner(m, k):
        for side in (1, 0):
            send(terms.at[m, lane_of(k, side, 1)], from_core.at[m, k, side], core_sem.at[m, k, side], to_core)

    def down_term(k, following=None):
        zk = z_of[k]
        hidden_t[...] = hidden[:, pl.ds(pl.multiple_of(zk * 2 * depth, depth), 2 * depth)].T

        @pl.loop(0, width // 256)
        def _(n):
            at = pl.ds(pl.multiple_of(n * 256, 256), 256)
            got = jnp.dot(hidden_t[...], cot[:, at], preferred_element_type=F32)
            if following is not None:
                start = z_of[following] * 2 * depth + n * (depth // 2)
                to = pl.ds(pl.multiple_of(start, depth // 2), depth // 2)
                for i in range(rows // 32):
                    act, slope = gelu_parts(pre[pl.ds(i * 32, 32), to])
                    hidden[pl.ds(i * 32, 32), to] = act.astype(BF16)
                    pre[pl.ds(i * 32, 32), to] = slope
            terms[1, pl.ds(zk * 4, 4), :, at] = got.astype(BF16).reshape(4, 2 * part_rows, 256)

        to_partner(1, k)

    def up_term(k):
        zk = z_of[k]
        own = pl.ds(pl.multiple_of(zk * depth, depth), depth)
        for h in (0, 1):
            @pl.loop(0, width // 512)
            def _(n):
                to = pl.ds(pl.multiple_of(h * width + n * 512, 512), 512)
                got = jnp.dot(normed_t[own], pre_grad[:, to], preferred_element_type=F32)
                at = pl.ds(pl.multiple_of(n * 512, 512), 512)
                terms[0, pl.ds(zk * 4, 4), pl.ds(h * part_rows, part_rows), at] = (
                    got.astype(BF16).reshape(4, part_rows, 512)
                )
        to_partner(0, k)

    def add(dst, *parts):
        @pl.loop(0, dst.shape[0] // 32)
        def _(i):
            at = pl.ds(pl.multiple_of(i * 32, 32), 32)
            total = parts[0][at].astype(F32)
            for part in parts[1:]:
                total = total + part[at].astype(F32)
            dst[at] = total.astype(dst.dtype)

    def chip_sum(m, k, side):
        mine = from_core.at[m, k, side]
        arrive(mine, core_sem.at[m, k, side])
        parts = [terms.at[m, lane_of(k, side, 0)], mine]
        if side == 0 and k in X_FIRST:
            arrive(from_x2.at[m, k], x2_sem.at[m, k])
            parts.append(from_x2.at[m, k])
        add(mine, *parts)
        if side == 1 and k in X_FIRST:
            send(mine, from_x2.at[m, k], x2_sem.at[m, k], to_x)
        else:
            send(from_core.at[m, k, side, half(other)], from_y.at[m, k, side], y_sem.at[m, k, side], to_y)

    def pair_sum(m, k, side):
        mine = from_y.at[m, k, side]
        arrive(mine, y_sem.at[m, k, side])
        parts = [from_core.at[m, k, side, half(y)], mine]
        if side == 0 and k not in X_FIRST:
            arrive(from_x.at[m, k], x_sem.at[m, k])
            parts.append(from_x.at[m, k])
        if side == 0 and k == 0:
            for j in (1, 2, 3):
                arrive(from_z.at[m, j], z_sem.at[m, j])
                parts.append(from_z.at[m, j])
            done = final.at[m, half(y)]
            add(done, *parts)
            send(done, done, final_sem.at[m], to_y)
            return
        add(mine, *parts)
        if side == 1:
            send(mine, from_x.at[m, k], x_sem.at[m, k], to_x)
        else:
            send(mine, from_z.at[m, k], z_sem.at[m, k], to_z[k])

    def mix(n):
        at = pl.ds(n * 256, 256)
        block = weights[1, :, :, at].reshape(2 * width, 256)
        got = jnp.dot(hidden[pl.ds(0, new_count)], block, preferred_element_type=F32)
        out_ref[:, at] = (fresh[:, at].astype(F32) + got).astype(BF16)

    def near(m):
        for h in (0, 1):
            pass_on(m, h, 0, 1, (to_core,))
        pass_on(m, y, 1, 0, (to_x, to_core))
        pass_on(m, other, 1, 0, (to_core,))

    def far(m):
        pass_on(m, y, 3, 0, (to_x, to_y, to_core))
        pass_on(m, y, 2, 0, (to_x, to_core))

    def cross(m, k):
        pass_on(m, y, k, 1, (to_y, to_core))

    def swap(m, k, side):
        pass_on(m, other, k, side, (to_core,))

    near(0)
    far(0)
    own_send(1)

    @pl.loop(0, 4)
    def _(i):
        at = pl.ds(pl.multiple_of(i * depth, depth), depth)
        normed_t[at] = normed[:, at].T

    cross(0, 1)
    cross(0, 3)
    swap(0, 3, 0)
    pre_slab(0, True)
    cross(0, 2)
    swap(0, 2, 0)
    swap(0, 1, 1)
    near(1)
    swap(0, 3, 1)
    pre_slab(1, False)
    swap(0, 2, 1)
    far(1)
    pre_slab(3, False)
    cross(1, 1)
    pre_slab(2, False)
    cross(1, 3)
    swap(1, 3, 0)
    act_slab(2)
    down_term(2, 3)
    cross(1, 2)
    swap(1, 2, 0)
    swap(1, 1, 1)
    swap(1, 3, 1)
    swap(1, 2, 1)
    down_term(3, 1)
    chip_sum(1, 2, 1)
    chip_sum(1, 3, 1)
    down_term(1, 0)
    chip_sum(1, 2, 0)
    chip_sum(1, 1, 1)
    down_term(0)
    chip_sum(1, 3, 0)
    pair_sum(1, 2, 1)
    chip_sum(1, 0, 1)
    back_slab(0)
    chip_sum(1, 1, 0)
    chip_sum(1, 0, 0)
    back_slab(1)
    pair_sum(1, 3, 0)
    pair_sum(1, 2, 0)
    back_slab(3)
    pair_sum(1, 0, 1)
    back_slab(2)
    up_term(2)
    pair_sum(1, 1, 0)
    up_term(3)
    chip_sum(0, 2, 1)
    chip_sum(0, 3, 1)
    up_term(1)
    chip_sum(0, 2, 0)
    chip_sum(0, 1, 1)
    up_term(0)
    chip_sum(0, 0, 1)
    chip_sum(0, 3, 0)
    pair_sum(0, 2, 1)
    chip_sum(0, 0, 0)
    chip_sum(0, 1, 0)
    pair_sum(1, 0, 0)
    mix(0)
    pair_sum(0, 3, 0)
    pair_sum(0, 0, 1)
    mix(1)
    pair_sum(0, 2, 0)
    pair_sum(0, 1, 0)
    mix(2)
    mix(3)
    arrive(final.at[1, half(other)], final_sem.at[1])
    down_ref[...] = final[1].astype(F32)
    pair_sum(0, 0, 0)
    arrive(final.at[0, half(other)], final_sem.at[0])
    for h in (0, 1):
        up_ref[:, pl.ds(h * width, width)] = final[0, pl.ds(h * part_rows, part_rows)].astype(F32)
    for copy in pending:
        copy.wait_send()


def fused_body(reservoir, send_rows, send_count, new_rows, w_up, w_down, ln_gain, grad_new, grad_old):
    groups, slots = send_rows.shape[1:]
    fresh_count, width = new_rows.shape
    hid = w_up.shape[1]
    rows = fresh_count + grad_old.shape[0]
    padded = -(-rows // 128) * 128
    chunk = w_down.shape[0]
    vmem = pl.BlockSpec(memory_space=pltpu.VMEM)
    anywhere = pl.BlockSpec(memory_space=pl.ANY)
    dma = pltpu.SemaphoreType.DMA
    held = lambda *shape: pltpu.VMEM(shape, BF16)
    return pl.pallas_call(
        fused_kernel,
        out_shape=(
            jax.ShapeDtypeStruct((fresh_count, width), BF16),
            jax.ShapeDtypeStruct(w_up.shape, F32),
            jax.ShapeDtypeStruct(w_down.shape, F32),
        ),
        in_specs=[vmem] * 5 + [anywhere] * 4,
        out_specs=(vmem,) * 3,
        scratch_shapes=[
            held(2, FUSED_LANES, chunk, width),
            held(*reservoir.shape),
            held(fresh_count, width),
            held(padded, width),
            held(groups, slots, width),
            held(groups, slots, width),
            held(padded, width),
            pltpu.VMEM((rows, hid), F32),
            held(padded, hid),
            held(padded, hid),
            held(width, padded),
            held(width // 2, padded),
            held(2, FUSED_LANES, chunk, width),
            held(2, 4, 2, chunk, width),
            held(2, 4, chunk, width),
            held(2, 4, 2, chunk // 2, width),
            held(2, 4, chunk // 2, width),
            held(2, 4, chunk // 2, width),
            held(2, chunk, width),
            dma((4,)),
            dma((112,)),
            dma((2, 2, FUSED_LANES)),
            dma(()),
            dma(()),
            dma((2, 4, 2)),
            dma((2, 4)),
            dma((2, 4, 2)),
            dma((2, 4)),
            dma((2, 4)),
            dma((2,)),
        ],
        compiler_params=pltpu.CompilerParams(
            collective_id=0, has_side_effects=True, vmem_limit_bytes=60 * 1024 * 1024
        ),
        cost_estimate=pl.CostEstimate(
            flops=10 * rows * width * hid, bytes_accessed=16 * 1024 * 1024, transcendentals=2 * rows * hid
        ),
    )(send_rows, send_count, ln_gain, w_up, w_down, reservoir, new_rows, grad_new, grad_old)


def solution(mesh):
    fused = mesh.shape["grp"] == FUSED_GROUPS and mesh.shape["dev"] == FUSED_LANES
    return jax.shard_map(
        fused_body if fused else plain_body,
        mesh=mesh,
        in_specs=(
            P(("grp", "dev"), None),
            P(("grp", "dev"), None, None),
            P(("grp", "dev"), None),
            P(("grp", "dev"), None),
            P("dev", None),
            P("dev", None),
            P(),
            P(("grp", "dev"), None),
            P(("grp", "dev"), None),
        ),
        out_specs=(P(("grp", "dev"), None), P("dev", None), P("dev", None)),
        check_vma=False,
    )
```
